128 devices in a mesh: seq: 32 (over y, z, core), mp: 4 (over x).
Axes of the slice: x: 4, y: 4, z: 4, core: 2. Of those that a mesh axis runs over, the one named last changes fastest.
Arguments:
- byte_states: bfloat16 [8192, 1024], P('seq'), may hold values from -6 to 6
- patch_lengths: int32 [32, 32], P('seq'), may hold values from 1 to 16, 256 in all within a row
- patch_owner: int32 [1024, 1], P('seq'), may hold values from 0 to 31; in each aligned block of 32 rows (0 to 31, 32 to 63, ...) at most 2 rows name the same one
- w_enc: bfloat16 [1024, 4096], P(None, 'mp'), may hold values from -0.5 to 0.5
- w_gate: bfloat16 [4096, 14336], P('mp', 'seq'), may hold values from -0.09375 to 0.09375
- w_lift: bfloat16 [4096, 14336], P('mp', 'seq'), may hold values from -0.09375 to 0.09375
- w_down: bfloat16 [14336, 4096], P('seq', 'mp'), may hold values from -0.046875 to 0.046875
- w_dec: bfloat16 [4096, 1024], P('mp'), may hold values from -0.09375 to 0.09375
- byte_cot: bfloat16 [8192, 1024], P('seq'), may hold values from -6 to 6
Outputs:
- byte_out: bfloat16 [8192, 1024], P('seq')
- byte_grad: bfloat16 [8192, 1024], P('seq')
- latent_states: bfloat16 [2048, 4096], P('seq', 'mp')
The draws below stay inside these ranges and needn't reach their ends.
Inputs may be any that keep to these rules, and one draw needn't show every extreme that they name: `patch_lengths`: each row sums to 256; the longest patch has exactly 16 bytes. `patch_owner`: among the patches of one byte shard (aligned blocks of 32 rows) no owner is named more than 2 times, a bound that some block reaches.
All inputs are finite; a program needn't handle non-finite values.
Results may differ from the reference program's by a relative error of at most 0.008.
Values may be sent and summed in bfloat16 or wider, within the bound.
No kernel may reach another device: no remote copies, remote signals or barrier semaphores. Data moves between devices by JAX's collectives and lax.ppermute only.
A program may use at most 128 MiB of HBM per device.

```python
import math
import jax
import jax.numpy as jnp
import numpy as np

DB = 1024
D = 4096
FF = 14336
MOST = 16
BYTES_DEV = 256
PATCH_DEV = 32
PATCHES = 1024
BYTES = 8192
SLOT = 2
OWN = 64
ROWS = 2048
N_SEQ = 32


def block_levels(key, dims, shards, low, largest):
    def one(position, blocks):
        draws = jax.random.uniform(jax.random.fold_in(jax.random.fold_in(key, 6), position), (blocks,), jnp.float32, low / len(shards), largest / len(shards))
        return jnp.repeat(jnp.exp(draws), dims[position] // blocks).reshape((-1,) + (1,) * (len(dims) - position - 1))

    loudness = one(*shards[0])
    for cut in shards[1:]:
        loudness = loudness * one(*cut)
    return loudness


def length_profile(number_of, total, limit, slope):
    weights = [(1 << 20) // math.isqrt(standing ** slope) + 1 for standing in range(2, number_of + 1)]
    rest, counts = total - limit - (number_of - 1), [1] * (number_of - 1)
    while rest > 0:
        candidates = [i for i in range(number_of - 1) if counts[i] < limit]
        pool, budget = sum([weights[i] for i in candidates]), rest
        for i in candidates:
            extra = min(limit - counts[i], max(1, budget * weights[i] // pool), rest)
            counts[i] = counts[i] + extra
            rest = rest - extra
    return np.array([limit] + counts)


def ragged(stream_key, amount, total, limit, skew):
    if amount == 2:
        one = jax.random.randint(stream_key, (), max(1, total - limit), min(limit, total - 1) + 1)
        return jnp.stack([one, total - one])
    sizes = jnp.asarray(length_profile(amount, total, limit, skew), jnp.int32)
    twos = (amount - 1) // 2
    giver, receiver = sizes[1:1 + 2 * twos:2], sizes[2:2 + 2 * twos:2]
    margin = jnp.minimum(giver - 1, limit - receiver)
    passed = jax.random.randint(jax.random.fold_in(stream_key, 1), (twos,), 0, 1 << 20) % (margin + 1)
    sizes = sizes.at[1:1 + 2 * twos:2].set(giver - passed).at[2:2 + 2 * twos:2].set(receiver + passed)
    return sizes[jax.random.permutation(jax.random.fold_in(stream_key, 2), amount)]


def assign_block(rng, own, number, rows, amount, top, reach, skew):
    order = jax.random.permutation(rng, amount)
    heavy_load, usual = portions_of(amount, rows * top, reach, skew, True), portions_of(amount, rows * top, reach, skew, False)
    places = jnp.arange(amount)

    def named(sizes, rotation):
        used = int((sizes > 0).sum())
        fixed = max(1, used // 4)
        passed = fixed + (places - fixed + rotation * (used - fixed)) % max(1, amount - fixed)
        return jnp.zeros((amount,), jnp.int32).at[order[jnp.where(places < fixed, places, passed)]].set(jnp.asarray(sizes, jnp.int32))

    sizes = jnp.where(number % 4 == 0, named(heavy_load, number // 4), named(usual, number - number // 4 - 1))
    mixed = jax.random.permutation(jax.random.fold_in(own, 3), amount)
    donor, taker = mixed[0:amount // 2 * 2:2], mixed[1:amount // 2 * 2:2]
    margin = jnp.minimum(sizes[donor] - 1, reach - sizes[taker]) // 2
    margin = jnp.where((donor == order[0]) | (taker == order[0]) | (sizes[taker] == 0), 0, jnp.maximum(margin, 0))
    passed = jax.random.randint(jax.random.fold_in(own, 4), (amount // 2,), 0, 1 << 20) % (margin + 1)
    sizes = sizes.at[donor].add(-passed).at[taker].add(passed)
    members = jnp.searchsorted(jnp.cumsum(sizes), jnp.arange(rows * top), side="right").astype(jnp.int32)
    listing = members.reshape(top, rows).T
    listing = listing[jax.random.permutation(jax.random.fold_in(own, 1), rows)]
    rotation = jax.random.randint(jax.random.fold_in(own, 2), (rows, 1), 0, top)
    return jnp.take_along_axis(listing, (jnp.arange(top)[None, :] + rotation) % top, axis=1)


def portions_of(count, total, limit, skew, full):
    loads = [(1 << 20) // math.isqrt(rank ** skew) + 1 for rank in range(1, count + 1)]
    largest = limit if full else min(limit, max(-(-total // count), total * loads[0] // sum(loads)))
    least = 1 if total - largest >= count - 1 else 0
    counts, spare = [largest] + [least] * (count - 1), total - largest - least * (count - 1)
    while spare > 0:
        candidates = [i for i in range(1, count) if counts[i] < largest] or [i for i in range(1, count) if counts[i] < limit]
        pool, remaining = sum([loads[i] for i in candidates]), spare
        for i in candidates:
            more = min(limit - counts[i], max(1, remaining * loads[i] // pool), spare)
            counts[i] = counts[i] + more
            spare = spare - more
    return np.array(counts)


def scatter_about(stream_key, dims, deviation, most, pieces=(), kind=jnp.bfloat16):
    values = jax.random.normal(stream_key, dims, jnp.float32) * deviation
    if len(pieces) > 0:
        values = block_levels(stream_key, dims, pieces, -0.22, 0.18) * values
    return jnp.clip(values, min=-most, max=most).astype(kind)


def setup_inputs(seed: int = 0) -> dict:
    key_list = jax.random.split(jax.random.key(seed), 10)
    byte_states = scatter_about(key_list[0], (BYTES, DB), 1.0, 6.0, ((0, 32),))
    patch_lengths = jax.vmap(lambda own: ragged(own, PATCH_DEV, BYTES_DEV, MOST, 2))(jax.random.split(key_list[1], N_SEQ)).reshape((N_SEQ, PATCH_DEV)).astype(jnp.int32)
    patch_owner_keys = jax.random.split(jax.random.fold_in(key_list[2], 1), PATCHES // PATCH_DEV)
    patch_owner_turns = jax.random.permutation(jax.random.fold_in(key_list[2], 3), PATCHES // PATCH_DEV)
    patch_owner = jax.vmap(lambda own, number: assign_block(jax.random.fold_in(key_list[2], 2), own, number, PATCH_DEV, N_SEQ, 1, SLOT, 2))(patch_owner_keys, patch_owner_turns).reshape((PATCHES, 1))
    w_enc = scatter_about(key_list[3], (DB, D), (DB // 8) ** -0.5, 0.5, ((1, 4),))
    w_gate = scatter_about(key_list[4], (D, FF), D ** -0.5, 0.09375, ((0, 4), (1, 32)))
    w_lift = scatter_about(key_list[5], (D, FF), D ** -0.5, 0.09375, ((0, 4), (1, 32)))
    w_down = scatter_about(key_list[6], (FF, D), FF ** -0.5, 0.046875, ((0, 32), (1, 4)))
    w_dec = scatter_about(key_list[7], (D, DB), D ** -0.5, 0.09375, ((0, 4),))
    byte_cot = scatter_about(key_list[8], (BYTES, DB), 1.0, 6.0, ((0, 32),))
    return dict(byte_states=byte_states, patch_lengths=patch_lengths, patch_owner=patch_owner, w_enc=w_enc, w_gate=w_gate, w_lift=w_lift, w_down=w_down, w_dec=w_dec, byte_cot=byte_cot)


def layout(patch_lengths, patch_owner):
    patch_ends = jnp.cumsum(patch_lengths, axis=1).astype(jnp.int32)
    positions = jnp.arange(BYTES_DEV, dtype=jnp.int32)
    local_patch = jnp.sum((patch_ends[:, None, :] <= positions[None, :, None]).astype(jnp.int32), axis=2).astype(jnp.int32)
    sources = jnp.arange(N_SEQ, dtype=jnp.int32)
    patch_id = (local_patch + sources[:, None] * PATCH_DEV).reshape(-1).astype(jnp.int32)
    owners = patch_owner.reshape(N_SEQ, PATCH_DEV).astype(jnp.int32)
    onehot = (owners[:, :, None] == sources[None, None, :]).astype(jnp.int32)
    ranks = jnp.sum((jnp.cumsum(onehot, axis=1).astype(jnp.int32) - 1) * onehot, axis=2).astype(jnp.int32)
    slots = (owners * OWN + sources[:, None] * SLOT + ranks).reshape(-1).astype(jnp.int32)
    return patch_id, slots


def reference(byte_states, patch_lengths, patch_owner, w_enc, w_gate, w_lift, w_down, w_dec, byte_cot):
    patch_id, slots = layout(patch_lengths, patch_owner)
    lengths = patch_lengths.reshape(-1).astype(jnp.float32)[:, None]
    pooled = (jax.ops.segment_sum(byte_states.astype(jnp.float32), patch_id, PATCHES) / lengths).astype(jnp.bfloat16)
    patch_rep = jnp.dot(pooled, w_enc, preferred_element_type=jnp.float32).astype(jnp.bfloat16)
    latent_in = jnp.zeros((ROWS, D), jnp.bfloat16).at[slots].set(patch_rep)
    gate_value = jnp.dot(latent_in, w_gate, preferred_element_type=jnp.float32)
    lift_value = jnp.dot(latent_in, w_lift, preferred_element_type=jnp.float32)
    hidden = (jax.nn.silu(gate_value) * lift_value).astype(jnp.bfloat16)
    latent_states = (latent_in.astype(jnp.float32) + jnp.dot(hidden, w_down, preferred_element_type=jnp.float32)).astype(jnp.bfloat16)
    decoded = jnp.dot(latent_states[slots], w_dec, preferred_element_type=jnp.float32)
    byte_out = (byte_states.astype(jnp.float32) + decoded[patch_id]).astype(jnp.bfloat16)
    patch_cot = jax.ops.segment_sum(byte_cot.astype(jnp.float32), patch_id, PATCHES).astype(jnp.bfloat16)
    grad_back = jnp.dot(patch_cot, w_dec.T, preferred_element_type=jnp.float32).astype(jnp.bfloat16)
    grad_own = jnp.zeros((ROWS, D), jnp.bfloat16).at[slots].set(grad_back)
    grad_hidden = jnp.dot(grad_own, w_down.T, preferred_element_type=jnp.float32)
    sigma = jax.nn.sigmoid(gate_value)
    grad_gate = (grad_hidden * lift_value * sigma * (1.0 + gate_value * (1.0 - sigma))).astype(jnp.bfloat16)
    grad_lift = (grad_hidden * gate_value * sigma).astype(jnp.bfloat16)
    grad_in = (grad_own.astype(jnp.float32) + jnp.dot(grad_gate, w_gate.T, preferred_element_type=jnp.float32) + jnp.dot(grad_lift, w_lift.T, preferred_element_type=jnp.float32)).astype(jnp.bfloat16)
    grad_pool = jnp.dot(grad_in[slots], w_enc.T, preferred_element_type=jnp.float32) / lengths
    byte_grad = (byte_cot.astype(jnp.float32) + grad_pool[patch_id]).astype(jnp.bfloat16)
    return byte_out, byte_grad, latent_states
```

```python
import functools

import jax
import jax.numpy as jnp
from jax import lax
from jax.experimental import pallas as pl
from jax.experimental.pallas import tpu as pltpu
from jax.sharding import Mesh
from jax.sharding import PartitionSpec as P

F32 = jnp.float32
BF16 = jnp.bfloat16
SEQ = ("y", "z", "c")
VMEM_LIMIT = 48 * 1024 * 1024


def swap_core(value):
    return lax.ppermute(value, "c", [(0, 1), (1, 0)])


def swap_x(value, k):
    return lax.ppermute(value, "x", [(i, i ^ k) for i in range(4)])


def swap_near(value, first):
    steps = (1, 3) if first else (3, 1)
    return lax.ppermute(
        value, ("c", "x"), [(c * 4 + x, c * 4 + (x ^ steps[c])) for c in range(2) for x in range(4)]
    )


def dot(a, b):
    return jnp.dot(a, b, preferred_element_type=F32)


def dot_t(a, b):
    return lax.dot_general(a, b, (((1,), (1,)), ((), ())), preferred_element_type=F32)


def call(body, outs, inputs, scalars=(), flops=0):
    specs = [pl.BlockSpec(memory_space=pltpu.SMEM)] * len(scalars)
    specs += [pl.BlockSpec(memory_space=pltpu.VMEM)] * len(inputs)
    moved = sum(v.size * v.dtype.itemsize for v in list(inputs) + list(outs))
    return pl.pallas_call(
        body,
        out_shape=outs,
        in_specs=specs,
        out_specs=[pl.BlockSpec(memory_space=pltpu.VMEM)] * len(outs),
        compiler_params=pltpu.CompilerParams(vmem_limit_bytes=VMEM_LIMIT),
        cost_estimate=pl.CostEstimate(flops=flops, bytes_accessed=moved, transcendentals=0),
    )(*scalars, *inputs)


def shape(dims, dtype):
    return jax.ShapeDtypeStruct(dims, dtype)


def bounds(lengths):
    count = lengths.shape[1]
    row = lax.broadcasted_iota(jnp.int32, (count, count), 0)
    column = lax.broadcasted_iota(jnp.int32, (count, count), 1)
    wide = jnp.broadcast_to(lengths, (count, count)).astype(F32)
    ends = jnp.sum(jnp.where(column <= row, wide, 0.0), axis=1, keepdims=True)
    size = jnp.sum(jnp.where(column == row, wide, 0.0), axis=1, keepdims=True)
    return ends - size, ends, size


def membership(lengths, length):
    starts, ends, size = bounds(lengths)
    count = lengths.shape[1]
    position = lax.broadcasted_iota(jnp.int32, (count, length), 1).astype(F32)
    inside = (position >= starts) & (position < ends)
    return jnp.where(inside, 1.0, 0.0).astype(BF16), size


def encode_kernel(forward, lengths, values, weight, rep, repeated):
    pooling, size = membership(lengths[...], values.shape[0])
    pooled = dot(pooling, values[...])
    if forward:
        result = dot((pooled / size).astype(BF16), weight[...])
    else:
        result = dot_t(pooled.astype(BF16), weight[...])
    result = result.astype(BF16)
    rep[...] = result
    for i in range(repeated.shape[0]):
        repeated[i] = result


def spread_kernel(transposed, offsets, near, far, weight, keep, send):
    multiply = dot_t if transposed else dot
    span = near.shape[0] // 4

    @pl.loop(0, 2)
    def _(t):
        off = pl.multiple_of(offsets[t], span)
        keep[t, 0] = multiply(near[pl.ds(off, span), :], weight[...])
        keep[t, 1] = multiply(far[pl.ds(off, span), :], weight[...])

    @pl.loop(0, 2)
    def _(t):
        off = pl.multiple_of(offsets[t + 2], span)
        send[t, 0] = multiply(near[pl.ds(off, span), :], weight[...]).astype(BF16)
        send[t, 1] = multiply(far[pl.ds(off, span), :], weight[...]).astype(BF16)


def down_kernel(transposed, offsets, own, second, others, weight, near, far):
    multiply = dot_t if transposed else dot
    span = near.shape[0] // 4
    blocks = [own, second, others.at[0], others.at[1]]
    for t, block in enumerate(blocks):
        off = pl.multiple_of(offsets[t], span)
        near[pl.ds(off, span), :] = multiply(block[0], weight[...]).astype(BF16)
        far[pl.ds(off, span), :] = multiply(block[1], weight[...]).astype(BF16)


def decode_kernel(forward, arrived, rep, weight, owners, *outs):
    total = rep[...].astype(F32)
    for i in range(arrived.shape[0]):
        total = total + arrived[i].astype(F32)
    states = total.astype(BF16)
    if forward:
        partial, outgoing = outs
        partial[...] = dot(states, weight[...]).astype(BF16)
        count = rep.shape[0]
        own_row = jnp.broadcast_to(owners[...], (count, count))
        row = lax.broadcasted_iota(jnp.int32, (count, count), 0)
        column = lax.broadcasted_iota(jnp.int32, (count, count), 1)
        own_column = jnp.sum(jnp.where(row == column, own_row, 0), axis=1, keepdims=True)
        same = jnp.where((own_column == own_row) & (row < column), 1, 0)
        targets = 2 * owners[...] + jnp.sum(same, axis=0, keepdims=True)
        slots = lax.broadcasted_iota(jnp.int32, (2 * count, count), 0)
        routing = jnp.where(slots == targets, 1.0, 0.0).astype(BF16)
        outgoing[...] = dot(routing, states).astype(BF16)
    else:
        (partial,) = outs
        partial[...] = dot_t(states, weight[...]).astype(BF16)


def finish_kernel(forward, lengths, values, own, one, two, three, out):
    total = (
        own[...].astype(F32) + one[...].astype(F32) + two[...].astype(F32) + three[...].astype(F32)
    )
    pooling, size = membership(lengths[...], values.shape[0])
    if not forward:
        total = total / size
    high = total.astype(BF16)
    low = (total - high.astype(F32)).astype(BF16)
    pick = (((0,), (0,)), ((), ()))
    spread = lax.dot_general(pooling, high, pick, preferred_element_type=F32)
    spread = spread + lax.dot_general(pooling, low, pick, preferred_element_type=F32)
    out[...] = (values[...].astype(F32) + spread).astype(BF16)


def gather_seq(repeated):
    near = lax.all_to_all(repeated, ("y", "z"), split_axis=0, concat_axis=0, tiled=True)
    near = near.reshape(-1, near.shape[2])
    return near, swap_core(near)


def scatter_x(keep, send):
    first = swap_near(send, True)
    second = swap_near((keep[1] + first[1].astype(F32)).astype(BF16), False)
    return keep[0] + first[0].astype(F32) + second.astype(F32)


def gather_x(block):
    second = swap_near(block, False)
    others = swap_near(jnp.stack([block, second]), True)
    return block, second, others


def scatter_seq(near, far):
    total = (near.astype(F32) + swap_core(far).astype(F32)).astype(BF16)
    total = total.reshape(16, -1, total.shape[1])
    return lax.all_to_all(total, ("y", "z"), split_axis=0, concat_axis=0, tiled=True)


def on_device(
    byte_states, patch_lengths, patch_owner, w_enc, w_gate, w_lift, w_down, w_dec, byte_cot
):
    patches = patch_lengths.shape[1]
    width = w_enc.shape[1]
    hid = w_gate.shape[1]
    span = 4 * patches
    x = lax.axis_index("x")
    core = lax.axis_index("c")
    step = jnp.where(core == 0, 1, 3)
    offsets = (jnp.stack([x, x ^ step ^ 2, x ^ step, x ^ 2]) * span).astype(jnp.int32)
    owners = patch_owner.reshape(1, patches)
    pair = jnp.concatenate([w_gate, w_lift], axis=1)
    enc_out = [shape((patches, width), BF16), shape((16, patches, width), BF16)]
    flops = 2 * patches * width * width

    patch_rep, repeated = call(
        functools.partial(encode_kernel, True), enc_out, [patch_lengths, byte_states, w_enc], flops=flops
    )
    near, far = gather_seq(repeated)

    def spread(transposed, near, far, weight, columns):
        return call(
            functools.partial(spread_kernel, transposed),
            [shape((2, 2, span, columns), F32), shape((2, 2, span, columns), BF16)],
            [near, far, weight],
            [offsets],
            flops=2 * 8 * span * width * columns,
        )

    def down(transposed, blocks, weight, columns):
        return call(
            functools.partial(down_kernel, transposed),
            [shape((4 * span, width), BF16)] * 2,
            [*blocks, weight],
            [offsets],
            flops=2 * 8 * span * width * columns,
        )

    keep, send = spread(False, near, far, pair, 2 * hid)
    byte_cot_in, send = lax.optimization_barrier((byte_cot, send))
    grad_back, repeated = call(
        functools.partial(encode_kernel, False), enc_out, [patch_lengths, byte_cot_in, w_dec], flops=flops
    )
    gates = scatter_x(keep, send)
    near, far = gather_seq(repeated)
    keep, send = spread(True, near, far, w_down, hid)

    gate, lift = gates[:, :, :hid], gates[:, :, hid:]
    sig = jax.nn.sigmoid(gate)
    silu = gate * sig
    hidden = (silu * lift).astype(BF16)
    hiddens = gather_x(hidden)
    grad_hidden = scatter_x(keep, send)
    grads = jnp.concatenate(
        [grad_hidden * lift * sig * (1.0 + gate * (1.0 - sig)), grad_hidden * silu], axis=2
    ).astype(BF16)
    grads = gather_x(grads)
    near, far = down(False, hiddens, w_down, hid)
    arrived = scatter_seq(near, far)
    decoded, outgoing = call(
        functools.partial(decode_kernel, True),
        [shape((patches, width), BF16), shape((2 * patches, width), BF16)],
        [arrived, patch_rep, w_dec, owners],
        flops=flops,
    )
    near, far = down(True, grads, pair, 2 * hid)
    arrived = scatter_seq(near, far)
    (grad_pool,) = call(
        functools.partial(decode_kernel, False),
        [shape((patches, width), BF16)],
        [arrived, grad_back, w_enc, owners],
        flops=flops,
    )
    latent = lax.all_to_all(outgoing, SEQ, split_axis=0, concat_axis=0, tiled=True)

    def finish(forward, values, partial):
        return call(
            functools.partial(finish_kernel, forward),
            [shape(values.shape, BF16)],
            [patch_lengths, values, partial] + [swap_x(partial, k) for k in (1, 2, 3)],
            flops=4 * patches * values.size,
        )[0]

    return finish(True, byte_states, decoded), finish(False, byte_cot, grad_pool), latent


def solution(mesh):
    fine = Mesh(mesh.devices.reshape(4, 4, 2, 4), ("y", "z", "c", "x"))
    return jax.shard_map(
        on_device,
        mesh=fine,
        in_specs=(
            P(SEQ, None),
            P(SEQ, None),
            P(SEQ, None),
            P(None, "x"),
            P("x", SEQ),
            P("x", SEQ),
            P(SEQ, "x"),
            P("x", None),
            P(SEQ, None),
        ),
        out_specs=(P(SEQ, None), P(SEQ, None), P(SEQ, "x")),
        check_vma=False,
    )
```

```python
import functools

import jax
import jax.numpy as jnp
from jax import lax
from jax.experimental import pallas as pl
from jax.experimental.pallas import tpu as pltpu
from jax.sharding import Mesh
from jax.sharding import PartitionSpec as P

F32 = jnp.float32
BF16 = jnp.bfloat16
SEQ = ("y", "z", "c")
VMEM_LIMIT = 48 * 1024 * 1024


def swap_core(value):
    return lax.ppermute(value, "c", [(0, 1), (1, 0)])


def swap_x(value, k):
    return lax.ppermute(value, "x", [(i, i ^ k) for i in range(4)])


def swap_near(value, first):
    steps = (1, 3) if first else (3, 1)
    return lax.ppermute(
        value, ("c", "x"), [(c * 4 + x, c * 4 + (x ^ steps[c])) for c in range(2) for x in range(4)]
    )


def swap_axis(axis, value, k):
    return lax.ppermute(value, axis, [(i, i ^ k) for i in range(4)])


def dot(a, b):
    return jnp.dot(a, b, preferred_element_type=F32)


def dot_t(a, b):
    return lax.dot_general(a, b, (((1,), (1,)), ((), ())), preferred_element_type=F32)


def call(body, outs, inputs, scalars=(), flops=0, scratch=()):
    specs = [pl.BlockSpec(memory_space=pltpu.SMEM)] * len(scalars)
    specs += [pl.BlockSpec(memory_space=pltpu.VMEM)] * len(inputs)
    moved = sum(v.size * v.dtype.itemsize for v in list(inputs) + list(outs))
    return pl.pallas_call(
        body,
        out_shape=outs,
        in_specs=specs,
        out_specs=[pl.BlockSpec(memory_space=pltpu.VMEM)] * len(outs),
        scratch_shapes=list(scratch),
        compiler_params=pltpu.CompilerParams(vmem_limit_bytes=VMEM_LIMIT),
        cost_estimate=pl.CostEstimate(flops=flops, bytes_accessed=moved, transcendentals=0),
    )(*scalars, *inputs)


def shape(dims, dtype):
    return jax.ShapeDtypeStruct(dims, dtype)


def bounds(lengths):
    count = lengths.shape[1]
    row = lax.broadcasted_iota(jnp.int32, (count, count), 0)
    column = lax.broadcasted_iota(jnp.int32, (count, count), 1)
    wide = jnp.broadcast_to(lengths, (count, count)).astype(F32)
    ends = jnp.sum(jnp.where(column <= row, wide, 0.0), axis=1, keepdims=True)
    size = jnp.sum(jnp.where(column == row, wide, 0.0), axis=1, keepdims=True)
    return ends - size, ends, size


def membership(lengths, length):
    starts, ends, size = bounds(lengths)
    count = lengths.shape[1]
    position = lax.broadcasted_iota(jnp.int32, (count, length), 1).astype(F32)
    inside = (position >= starts) & (position < ends)
    return jnp.where(inside, 1.0, 0.0).astype(BF16), size


def pool_kernel(lengths, states, cots, repeated, pooled, pooled_cot):
    pooling, size = membership(lengths[...], states.shape[0])
    width = states.shape[1]
    pooled[...] = (dot(pooling, states[...]) / size).astype(BF16)
    pooled_cot[...] = dot(pooling, cots[...]).astype(BF16)
    for i in range(repeated.shape[0]):
        repeated[i, :, :width] = pooled[...]
        repeated[i, :, width:] = pooled_cot[...]


def product_kernel(offsets, w_enc, w_gate, w_lift, w_down, w_dec, keep, send, whole):
    hid = w_gate.shape[0]
    part = hid // 4
    whole[:hid] = dot_t(w_gate[...], w_enc[...]).astype(BF16)
    whole[hid : 2 * hid] = dot_t(w_lift[...], w_enc[...]).astype(BF16)
    whole[2 * hid :] = dot(w_down[...], w_dec[...]).astype(BF16)
    for k in range(4):
        out = keep if k < 2 else send
        for i in range(3):
            place = pl.multiple_of(offsets[k] + i * hid, 16)
            to = (k % 2) * 3 * part + i * part
            out[to : to + part] = whole[pl.ds(place, part), :]


def encode_kernel(pooled, cot, w_enc, w_dec, rep, back):
    rep[...] = dot(pooled[...], w_enc[...]).astype(BF16)
    back[...] = dot_t(dot_t(cot[...], w_dec[...]).astype(BF16), w_enc[...])


def hidden_rows(rows, products):
    part = products.shape[0] // 3
    width = products.shape[1]
    both = dot_t(products[: 2 * part], rows[:, :width])
    gate, lift = both[:part], both[part:]
    grad_hidden = dot_t(products[2 * part :], rows[:, width:])
    sig = 1.0 / (1.0 + jnp.exp(-gate))
    silu = gate * sig
    grad_gate = grad_hidden * lift * sig * (1.0 + gate * (1.0 - sig))
    grads = jnp.concatenate([grad_gate, grad_hidden * silu], axis=0).astype(BF16)
    return (silu * lift).astype(BF16), grads


def near_kernel(rows, products, hidden, grads):
    hidden[...], grads[...] = hidden_rows(rows[...], products[...])


def far_kernel(rows, products, near_hidden, hidden, partial):
    half = near_hidden.shape[1]
    part = products.shape[0] // 3
    hidden[:, :half] = near_hidden[...]
    hidden[:, half:], grads = hidden_rows(rows[...], products[...])
    partial[...] = dot(grads.T, products[: 2 * part]).astype(BF16)


def place_blocks(blocks, whole, outs):
    patches = whole.shape[0] // 16
    for k, out in enumerate(outs):
        for i in range(4):
            place = pl.multiple_of(blocks[4 * k + i], patches)
            out[i * patches : (i + 1) * patches] = whole[pl.ds(place, patches), :]


def near_grad_kernel(blocks, grads, products, other, *rest):
    whole = rest[-1]
    total = dot(grads[...].T, products[: grads.shape[0]]) + other[...].astype(F32)
    whole[...] = total.astype(BF16)
    place_blocks(blocks, whole, rest[:-1])


def down_far_kernel(offsets, own, one, two, three, w_down, out, stack):
    part, span = own.shape[0], out.shape[0]
    for k, block in enumerate((own, one, two, three)):
        stack[pl.ds(pl.multiple_of(offsets[k], 16), part), :] = block[:, span:]
    out[...] = dot(stack[...].T, w_down[...]).astype(BF16)


def down_near_kernel(offsets, blocks, own, one, two, three, w_down, other, *rest):
    stack, whole = rest[-2:]
    part, span = own.shape[0], other.shape[0]
    for k, block in enumerate((own, one, two, three)):
        stack[pl.ds(pl.multiple_of(offsets[k], 16), part), :] = block[:, :span]
    total = dot(stack[...].T, w_down[...]) + other[...].astype(F32)
    whole[...] = total.astype(BF16)
    place_blocks(blocks, whole, rest[:-2])


def add_kernel(own, one, two, three, *outs):
    total = (
        own[...].astype(F32) + one[...].astype(F32) + two[...].astype(F32) + three[...].astype(F32)
    )
    patches = own.shape[0] // 4
    for i, out in enumerate(outs):
        out[...] = total[i * patches : (i + 1) * patches].astype(out.dtype)


def decode_kernel(own, one, two, three, rep, weight, owners, partial, outgoing):
    total = own[...] + one[...].astype(F32) + two[...].astype(F32) + three[...].astype(F32)
    total = total + rep[...].astype(F32)
    states = total.astype(BF16)
    partial[...] = dot(states, weight[...]).astype(BF16)
    count = rep.shape[0]
    own_row = jnp.broadcast_to(owners[...], (count, count))
    row = lax.broadcasted_iota(jnp.int32, (count, count), 0)
    column = lax.broadcasted_iota(jnp.int32, (count, count), 1)
    own_column = jnp.sum(jnp.where(row == column, own_row, 0), axis=1, keepdims=True)
    same = jnp.where((own_column == own_row) & (row < column), 1, 0)
    targets = 2 * owners[...] + jnp.sum(same, axis=0, keepdims=True)
    slots = lax.broadcasted_iota(jnp.int32, (2 * count, count), 0)
    routing = jnp.where(slots == targets, 1.0, 0.0).astype(BF16)
    outgoing[...] = dot(routing, states).astype(BF16)


def grad_kernel(own, one, two, three, back, partial):
    total = own[...] + one[...].astype(F32) + two[...].astype(F32) + three[...].astype(F32)
    partial[...] = (total + back[...]).astype(BF16)


def finish_kernel(forward, lengths, values, own, one, two, three, out):
    total = (
        own[...].astype(F32) + one[...].astype(F32) + two[...].astype(F32) + three[...].astype(F32)
    )
    pooling, size = membership(lengths[...], values.shape[0])
    if not forward:
        total = total / size
    high = total.astype(BF16)
    low = (total - high.astype(F32)).astype(BF16)
    pick = (((0,), (0,)), ((), ()))
    spread = lax.dot_general(pooling, high, pick, preferred_element_type=F32)
    spread = spread + lax.dot_general(pooling, low, pick, preferred_element_type=F32)
    out[...] = (values[...].astype(F32) + spread).astype(BF16)


def on_device(
    byte_states, patch_lengths, patch_owner, w_enc, w_gate, w_lift, w_down, w_dec, byte_cot
):
    patches = patch_lengths.shape[1]
    width = byte_states.shape[1]
    latent = w_enc.shape[1]
    hid = w_gate.shape[1]
    part = hid // 4
    group = 16 * patches
    x, y, z = lax.axis_index("x"), lax.axis_index("y"), lax.axis_index("z")
    step = jnp.where(lax.axis_index("c") == 0, 1, 3)
    halving = (jnp.stack([x, x ^ step ^ 2, x ^ step, x ^ 2]) * part).astype(jnp.int32)
    offsets = (jnp.stack([x, x ^ 1, x ^ 2, x ^ 3]) * part).astype(jnp.int32)
    near_z, near_y = z ^ jnp.arange(4), y ^ jnp.arange(4)
    blocks = ((near_y[None, :] * 4 + near_z[:, None]) * patches).reshape(16).astype(jnp.int32)
    owners = patch_owner.reshape(1, patches)
    w_gate, w_lift = w_gate.T, w_lift.T

    repeated, pooled, pooled_cot = call(
        pool_kernel,
        [shape((16, patches, 2 * width), BF16)] + [shape((patches, width), BF16)] * 2,
        [patch_lengths, byte_states, byte_cot],
        flops=4 * patches * byte_states.size,
    )
    near = lax.all_to_all(repeated, ("y", "z"), split_axis=0, concat_axis=0, tiled=True)
    near = near.reshape(group, 2 * width)
    pooled, w_gate = lax.optimization_barrier((pooled, w_gate))
    keep, send = call(
        product_kernel,
        [shape((6 * part, width), BF16)] * 2,
        [w_enc, w_gate, w_lift, w_down, w_dec],
        [halving],
        flops=6 * hid * width * latent,
        scratch=[pltpu.VMEM((3 * hid, width), BF16)],
    )
    patch_rep, back = call(
        encode_kernel,
        [shape((patches, latent), BF16), shape((patches, width), F32)],
        [pooled, pooled_cot, w_enc, w_dec],
        flops=6 * patches * width * latent,
    )
    first = swap_near(send, True)
    half = 3 * part
    second = swap_near((keep[half:].astype(F32) + first[half:].astype(F32)).astype(BF16), False)
    products = (keep[:half].astype(F32) + first[:half].astype(F32) + second.astype(F32)).astype(BF16)
    far = swap_core(near)
    flops = 2 * group * width * 3 * part
    near_hidden, near_grads = call(
        near_kernel,
        [shape((part, group), BF16), shape((2 * part, group), BF16)],
        [near, products],
        flops=flops,
    )
    hidden, far_partial = call(
        far_kernel,
        [shape((part, 2 * group), BF16), shape((group, width), BF16)],
        [far, products, near_hidden],
        flops=flops + 4 * group * width * part,
    )
    hiddens = [hidden] + [swap_x(hidden, k) for k in (1, 2, 3)]
    pieces = [shape((4 * patches, width), BF16)] * 4

    def over_z(own, *sends):
        return [own] + [swap_axis("z", send, k + 1) for k, send in enumerate(sends)]

    def over_y(terms):
        own, *sends = call(
            add_kernel,
            [shape((patches, width), F32)] + [shape((patches, width), BF16)] * 3,
            terms,
            flops=4 * terms[0].size,
        )
        return [own] + [swap_axis("y", send, k + 1) for k, send in enumerate(sends)]

    terms = call(
        near_grad_kernel,
        pieces,
        [near_grads, products, swap_core(far_partial)],
        [blocks],
        flops=4 * group * width * part,
        scratch=[pltpu.VMEM((group, width), BF16)],
    )
    terms = over_z(*terms)
    hiddens, terms = lax.optimization_barrier((hiddens, terms))
    terms = over_y(terms)
    (far,) = call(
        down_far_kernel,
        [shape((group, latent), BF16)],
        [*hiddens, w_down],
        [offsets],
        flops=2 * group * latent * hid,
        scratch=[pltpu.VMEM((hid, group), BF16)],
    )
    (grad_pool,) = call(
        grad_kernel, [shape((patches, width), BF16)], [*terms, back], flops=4 * back.size
    )
    terms = call(
        down_near_kernel,
        pieces,
        [*hiddens, w_down, swap_core(far)],
        [offsets, blocks],
        flops=2 * group * latent * hid,
        scratch=[pltpu.VMEM((hid, group), BF16), pltpu.VMEM((group, latent), BF16)],
    )
    terms = over_y(over_z(*terms))
    decoded, outgoing = call(
        decode_kernel,
        [shape((patches, width), BF16), shape((2 * patches, latent), BF16)],
        [*terms, patch_rep, w_dec, owners],
        flops=2 * patches * width * latent,
    )
    latent_states = lax.all_to_all(outgoing, SEQ, split_axis=0, concat_axis=0, tiled=True)

    def finish(forward, values, partial):
        return call(
            functools.partial(finish_kernel, forward),
            [shape(values.shape, BF16)],
            [patch_lengths, values, partial] + [swap_x(partial, k) for k in (1, 2, 3)],
            flops=4 * patches * values.size,
        )[0]

    byte_out = finish(True, byte_states, decoded)
    return byte_out, finish(False, byte_cot, grad_pool), latent_states


def solution(mesh):
    fine = Mesh(mesh.devices.reshape(4, 4, 2, 4), ("y", "z", "c", "x"))
    return jax.shard_map(
        on_device,
        mesh=fine,
        in_specs=(
            P(SEQ, None),
            P(SEQ, None),
            P(SEQ, None),
            P(None, "x"),
            P("x", SEQ),
            P("x", SEQ),
            P(SEQ, "x"),
            P("x", None),
            P(SEQ, None),
        ),
        out_specs=(P(SEQ, None), P(SEQ, None), P(SEQ, "x")),
        check_vma=False,
    )
```

```python
import functools

import jax
import jax.numpy as jnp
from jax import lax
from jax.experimental import pallas as pl
from jax.experimental.pallas import tpu as pltpu
from jax.sharding import Mesh
from jax.sharding import PartitionSpec as P

F32 = jnp.float32
BF16 = jnp.bfloat16
SEQ = ("y", "z", "c")
VMEM_LIMIT = 20 * 1024 * 1024


def swap_core(value):
    return lax.ppermute(value, "c", [(0, 1), (1, 0)])


def swap_x(value, k):
    return lax.ppermute(value, "x", [(i, i ^ k) for i in range(4)])


def swap_near(value, first):
    steps = (1, 3) if first else (3, 1)
    return lax.ppermute(
        value, ("c", "x"), [(c * 4 + x, c * 4 + (x ^ steps[c])) for c in range(2) for x in range(4)]
    )


def swap_axis(axis, value, k):
    return lax.ppermute(value, axis, [(i, i ^ k) for i in range(4)])


def dot(a, b):
    return jnp.dot(a, b, preferred_element_type=F32)


def dot_t(a, b):
    return lax.dot_general(a, b, (((1,), (1,)), ((), ())), preferred_element_type=F32)


def call(body, outs, inputs, scalars=(), flops=0, scratch=(), outside=False):
    specs = [pl.BlockSpec(memory_space=pltpu.SMEM)] * len(scalars)
    specs += [pl.BlockSpec(memory_space=pl.ANY if outside else pltpu.VMEM)] * len(inputs)
    moved = sum(v.size * v.dtype.itemsize for v in list(inputs) + list(outs))
    return pl.pallas_call(
        body,
        out_shape=outs,
        in_specs=specs,
        out_specs=[pl.BlockSpec(memory_space=pltpu.VMEM)] * len(outs),
        scratch_shapes=list(scratch),
        compiler_params=pltpu.CompilerParams(vmem_limit_bytes=VMEM_LIMIT),
        cost_estimate=pl.CostEstimate(flops=flops, bytes_accessed=moved, transcendentals=0),
    )(*scalars, *inputs)


def shape(dims, dtype):
    return jax.ShapeDtypeStruct(dims, dtype)


def bounds(lengths):
    count = lengths.shape[1]
    row = lax.broadcasted_iota(jnp.int32, (count, count), 0)
    column = lax.broadcasted_iota(jnp.int32, (count, count), 1)
    wide = jnp.broadcast_to(lengths, (count, count)).astype(F32)
    ends = jnp.sum(jnp.where(column <= row, wide, 0.0), axis=1, keepdims=True)
    size = jnp.sum(jnp.where(column == row, wide, 0.0), axis=1, keepdims=True)
    return ends - size, ends, size


def membership(lengths, length):
    starts, ends, size = bounds(lengths)
    count = lengths.shape[1]
    position = lax.broadcasted_iota(jnp.int32, (count, length), 1).astype(F32)
    inside = (position >= starts) & (position < ends)
    return jnp.where(inside, 1.0, 0.0).astype(BF16), size


def pool_kernel(lengths, states, pooled):
    pooling, size = membership(lengths[...], states.shape[0])
    pooled[...] = (dot(pooling, states[...]) / size).astype(BF16)


def pool_cot_kernel(lengths, cots, pooled):
    pooling, _ = membership(lengths[...], cots.shape[0])
    pooled[...] = dot(pooling, cots[...]).astype(BF16)


def stack_kernel(own, one, two, three, out):
    span = own.shape[0]
    for k, block in enumerate((own, one, two, three)):
        out[k * span : (k + 1) * span] = block[...]


def cut_products(count, offsets, whole, keep, send):
    part = keep.shape[0] // (2 * count)
    for k in range(4):
        out = keep if k < 2 else send
        for i in range(count):
            place = pl.multiple_of(offsets[k] + i * 4 * part, 16)
            to = (k % 2) * count * part + i * part
            out[to : to + part] = whole[pl.ds(place, part), :]


def gate_product_kernel(
    offsets, enc_hbm, gate_hbm, lift_hbm, keep, send, w_enc, w_gate, w_lift, whole, sems
):
    copies = [
        pltpu.make_async_copy(source, target, sems.at[i])
        for i, (source, target) in enumerate(
            ((enc_hbm, w_enc), (gate_hbm, w_gate), (lift_hbm, w_lift))
        )
    ]
    for copy in copies:
        copy.start()
    hid = w_gate.shape[0]
    copies[0].wait()
    copies[1].wait()
    whole[:hid] = dot_t(w_gate[...], w_enc[...]).astype(BF16)
    copies[2].wait()
    whole[hid:] = dot_t(w_lift[...], w_enc[...]).astype(BF16)
    cut_products(2, offsets, whole, keep, send)


def down_product_kernel(offsets, down_hbm, dec_hbm, keep, send, w_down, w_dec, whole, sems):
    copies = [
        pltpu.make_async_copy(down_hbm, w_down, sems.at[0]),
        pltpu.make_async_copy(dec_hbm, w_dec, sems.at[1]),
    ]
    for copy in copies:
        copy.start()
    for copy in copies:
        copy.wait()
    whole[...] = dot(w_down[...], w_dec[...]).astype(BF16)
    cut_products(1, offsets, whole, keep, send)


def halve_kernel(keep, first, own, send):
    half = own.shape[0]
    own[...] = keep[:half].astype(F32) + first[:half].astype(F32)
    send[...] = (keep[half:].astype(F32) + first[half:].astype(F32)).astype(BF16)


def encode_kernel(pooled, cot, w_enc, w_dec, rep, back):
    rep[...] = dot(pooled[...], w_enc[...]).astype(BF16)
    back[...] = dot_t(dot_t(cot[...], w_dec[...]).astype(BF16), w_enc[...])


def hidden_rows(rows, products):
    both = dot_t(products[...], jnp.concatenate([block[...] for block in rows], axis=0))
    part = both.shape[0] // 2
    gate, lift = both[:part], both[part:]
    hidden = gate * (1.0 / (1.0 + jnp.exp(-gate))) * lift
    return both, hidden.astype(BF16)


def near_kernel(r0, r1, r2, r3, own, second, products, gates, hidden):
    products[...] = (own[...] + second[...].astype(F32)).astype(BF16)
    gates[...], hidden[...] = hidden_rows((r0, r1, r2, r3), products)


def far_kernel(r0, r1, r2, r3, products, near_hidden, gates, hidden):
    half = near_hidden.shape[1]
    hidden[:, :half] = near_hidden[...]
    gates[...], hidden[:, half:] = hidden_rows((r0, r1, r2, r3), products)


def grad_rows(rows, down, gates):
    patches = rows[0].shape[0] // 4
    pieces = [rows[z][y * patches : (y + 1) * patches, :] for y in range(4) for z in range(4)]
    grad_hidden = dot_t(down, jnp.concatenate(pieces, axis=0))
    part = gates.shape[0] // 2
    gate, lift = gates[:part], gates[part:]
    sig = 1.0 / (1.0 + jnp.exp(-gate))
    grad_gate = grad_hidden * lift * sig * (1.0 + gate * (1.0 - sig))
    return jnp.concatenate([grad_gate, grad_hidden * (gate * sig)], axis=0).astype(BF16)


def grad_far_kernel(r0, r1, r2, r3, own, second, products, gates, down, partial):
    down[...] = (own[...] + second[...].astype(F32)).astype(BF16)
    grads = grad_rows((r0, r1, r2, r3), down[...], gates)
    partial[...] = dot(grads.T, products[...]).astype(BF16)


def place_blocks(total, outs):
    patches = total.shape[0] // 16
    for z, out in enumerate(outs):
        for y in range(4):
            place = (4 * y + z) * patches
            out[y * patches : (y + 1) * patches] = total[place : place + patches].astype(BF16)


def grad_near_kernel(r0, r1, r2, r3, down, products, gates, other, *outs):
    grads = grad_rows((r0, r1, r2, r3), down[...], gates)
    place_blocks(dot(grads.T, products[...]) + other[...].astype(F32), outs)


def down_far_kernel(offsets, own, one, two, three, w_down, out, stack):
    part, span = own.shape[0], out.shape[0]
    for k, block in enumerate((own, one, two, three)):
        stack[pl.ds(pl.multiple_of(offsets[k], 16), part), :] = block[:, span:]
    out[...] = dot(stack[...].T, w_down[...]).astype(BF16)


def down_near_kernel(offsets, own, one, two, three, w_down, other, *rest):
    stack = rest[-1]
    part, span = own.shape[0], other.shape[0]
    for k, block in enumerate((own, one, two, three)):
        stack[pl.ds(pl.multiple_of(offsets[k], 16), part), :] = block[:, :span]
    place_blocks(dot(stack[...].T, w_down[...]) + other[...].astype(F32), rest[:-1])


def add_kernel(own, one, two, three, *outs):
    total = (
        own[...].astype(F32) + one[...].astype(F32) + two[...].astype(F32) + three[...].astype(F32)
    )
    patches = own.shape[0] // 4
    for i, out in enumerate(outs):
        out[...] = total[i * patches : (i + 1) * patches].astype(out.dtype)


def decode_kernel(me, own, one, two, three, rep, weight, owners, partial, *outs):
    total = own[...] + one[...].astype(F32) + two[...].astype(F32) + three[...].astype(F32)
    states = (total + rep[...].astype(F32)).astype(BF16)
    partial[...] = dot(states, weight[...]).astype(BF16)
    count = rep.shape[0]
    own_row = jnp.broadcast_to(owners[...], (count, count))
    row = lax.broadcasted_iota(jnp.int32, (count, count), 0)
    column = lax.broadcasted_iota(jnp.int32, (count, count), 1)
    own_column = jnp.sum(jnp.where(row == column, own_row, 0), axis=1, keepdims=True)
    same = jnp.where((own_column == own_row) & (row < column), 1, 0)
    rank = jnp.sum(same, axis=0, keepdims=True)
    owner = owners[...]
    owner_y, owner_z, owner_c = owner >> 3, (owner >> 1) & 3, owner & 1
    targets = (((owner_z ^ me[1]) * 4 + (owner_y ^ me[0])) * 2 + (owner_c ^ me[2])) * 2 + rank
    slots = lax.broadcasted_iota(jnp.int32, (2 * count, count), 0)
    routing = jnp.where(slots == targets, 1.0, 0.0).astype(BF16)
    outgoing = dot(routing, states).astype(BF16)
    for k, out in enumerate(outs):
        out[...] = outgoing[k * count // 2 : (k + 1) * count // 2]


def move_rows(source_of, blocks):
    rows = jnp.concatenate([block[...] for block in blocks], axis=0)
    count = rows.shape[0]
    to = lax.broadcasted_iota(jnp.int32, (count, count), 0)
    source = lax.broadcasted_iota(jnp.int32, (count, count), 1)
    moved = jnp.where(source == source_of(to), 1.0, 0.0).astype(BF16)
    return dot(moved, rows).astype(BF16)


def route_y_kernel(own, one, two, three, *outs):
    moved = move_rows(
        lambda d: ((d >> 2) & 3) * 16 + (d >> 4) * 4 + (d & 3), (own, one, two, three)
    )
    for k, out in enumerate(outs):
        out[...] = moved[k * 16 : (k + 1) * 16]


def route_core_kernel(own, one, two, three, *outs):
    moved = move_rows(
        lambda d: ((d >> 1) & 15) * 4 + (d >> 5) * 2 + (d & 1), (own, one, two, three)
    )
    for k, out in enumerate(outs):
        out[...] = moved[k * 32 : (k + 1) * 32]


def route_end_kernel(me, own, other, out):
    out[...] = move_rows(
        lambda d: (((d >> 1) & 1) ^ me[2]) * 32
        + ((d >> 4) ^ me[0]) * 8
        + (((d >> 2) & 3) ^ me[1]) * 2
        + (d & 1),
        (own, other),
    )


def grad_kernel(own, one, two, three, back, partial):
    total = own[...] + one[...].astype(F32) + two[...].astype(F32) + three[...].astype(F32)
    partial[...] = (total + back[...]).astype(BF16)


def finish_kernel(forward, lengths, values, own, one, two, three, out):
    total = (
        own[...].astype(F32) + one[...].astype(F32) + two[...].astype(F32) + three[...].astype(F32)
    )
    pooling, size = membership(lengths[...], values.shape[0])
    if not forward:
        total = total / size
    high = total.astype(BF16)
    low = (total - high.astype(F32)).astype(BF16)
    pick = (((0,), (0,)), ((), ()))
    spread = lax.dot_general(pooling, high, pick, preferred_element_type=F32)
    spread = spread + lax.dot_general(pooling, low, pick, preferred_element_type=F32)
    out[...] = (values[...].astype(F32) + spread).astype(BF16)


def on_device(
    byte_states, patch_lengths, patch_owner, w_enc, w_gate, w_lift, w_down, w_dec, byte_cot
):
    patches = patch_lengths.shape[1]
    width = byte_states.shape[1]
    latent = w_enc.shape[1]
    hid = w_gate.shape[1]
    part = hid // 4
    group = 16 * patches
    x, y, z, core = [lax.axis_index(axis) for axis in ("x", "y", "z", "c")]
    step = jnp.where(core == 0, 1, 3)
    halving = (jnp.stack([x, x ^ step ^ 2, x ^ step, x ^ 2]) * part).astype(jnp.int32)
    offsets = (jnp.stack([x, x ^ 1, x ^ 2, x ^ 3]) * part).astype(jnp.int32)
    me = jnp.stack([y, z, core]).astype(jnp.int32)
    owners = patch_owner.reshape(1, patches)
    w_gate, w_lift = w_gate.T, w_lift.T

    def after(value, token):
        return lax.optimization_barrier((value, token))[0]

    def over(axis, own, *sends):
        sends = sends or (own,) * 3
        return [own] + [swap_axis(axis, send, k + 1) for k, send in enumerate(sends)]

    def products_of(body, weights, count):
        return call(
            body,
            [shape((2 * count * part, width), BF16)] * 2,
            weights,
            [halving],
            flops=2 * count * hid * width * latent,
            scratch=[pltpu.VMEM(w.shape, BF16) for w in weights]
            + [pltpu.VMEM((count * hid, width), BF16), pltpu.SemaphoreType.DMA((len(weights),))],
            outside=True,
        )

    def halve(keep, first):
        own, send = call(
            halve_kernel,
            [shape((keep.shape[0] // 2, width), F32), shape((keep.shape[0] // 2, width), BF16)],
            [keep, first],
            flops=2 * keep.size,
        )
        return own, swap_near(send, False)

    def pool(body, values):
        return call(
            body,
            [shape((patches, width), BF16)],
            [patch_lengths, values],
            flops=2 * patches * values.size,
        )[0]

    def gather(rows, first_axis, second_axis):
        (group,) = call(
            stack_kernel,
            [shape((4 * patches, width), BF16)],
            over(first_axis, rows),
            flops=4 * rows.size,
        )
        near = over(second_axis, group)
        return group, near, [swap_core(block) for block in near]

    keep, send = products_of(gate_product_kernel, [w_enc, w_gate, w_lift], 2)
    first = swap_near(send, True)
    pooled = pool(pool_kernel, after(byte_states, send))
    z_rows, near, far = gather(pooled, "z", "y")
    pooled_cot = pool(pool_cot_kernel, after(byte_cot, pooled))
    _, near_cot, far_cot = gather(after(pooled_cot, z_rows), "y", "z")
    down_keep, down_send = products_of(down_product_kernel, [w_down, w_dec], 1)
    own, second = halve(keep, first)
    down_first = swap_near(after(down_send, second), True)
    flops = 4 * group * width * part
    products, near_gates, near_hidden = call(
        near_kernel,
        [
            shape((2 * part, width), BF16),
            shape((2 * part, group), F32),
            shape((part, group), BF16),
        ],
        [*near, own, second],
        flops=flops,
    )
    far_gates, hidden = call(
        far_kernel,
        [shape((2 * part, group), F32), shape((part, 2 * group), BF16)],
        [*far, products, near_hidden],
        flops=flops,
    )
    hiddens = [hidden] + [swap_x(hidden, k) for k in (1, 2, 3)]
    patch_rep, back = call(
        encode_kernel,
        [shape((patches, latent), BF16), shape((patches, width), F32)],
        [pooled, pooled_cot, w_enc, w_dec],
        flops=6 * patches * width * latent,
    )
    hiddens, patch_rep, back = lax.optimization_barrier((hiddens, patch_rep, back))
    down_own, down_second = halve(down_keep, down_first)
    down, far_partial = call(
        grad_far_kernel,
        [shape((part, width), BF16), shape((group, width), BF16)],
        [*far_cot, down_own, down_second, products, far_gates],
        flops=flops,
    )
    pieces = [shape((4 * patches, width), BF16)] * 4

    def sum_seq(terms):
        own, *sends = call(
            add_kernel,
            [shape((patches, width), F32)] + [shape((patches, width), BF16)] * 3,
            over("z", *terms),
            flops=16 * patches * width,
        )
        return over("y", own, *sends)

    (far_rows,) = call(
        down_far_kernel,
        [shape((group, latent), BF16)],
        [*hiddens, w_down],
        [offsets],
        flops=2 * group * latent * hid,
        scratch=[pltpu.VMEM((hid, group), BF16)],
    )
    terms = call(
        down_near_kernel,
        pieces,
        [*hiddens, w_down, swap_core(far_rows)],
        [offsets],
        flops=2 * group * latent * hid,
        scratch=[pltpu.VMEM((hid, group), BF16)],
    )
    decoded, *outgoing = call(
        decode_kernel,
        [shape((patches, width), BF16)] + [shape((patches // 2, latent), BF16)] * 4,
        [*sum_seq(terms), patch_rep, w_dec, owners],
        [me],
        flops=2 * patches * width * latent,
    )
    terms = call(
        grad_near_kernel,
        pieces,
        [*near_cot, down, products, near_gates, swap_core(far_partial)],
        flops=flops,
    )
    (grad_pool,) = call(
        grad_kernel, [shape((patches, width), BF16)], [*sum_seq(terms), back], flops=4 * back.size
    )
    quarter, half = shape((patches // 2, latent), BF16), shape((patches, latent), BF16)
    outgoing = call(route_y_kernel, [quarter] * 4, over("z", *outgoing), flops=8 * patch_rep.size)
    mine, others = call(route_core_kernel, [half] * 2, over("y", *outgoing), flops=8 * patch_rep.size)
    (latent_states,) = call(
        route_end_kernel,
        [shape((2 * patches, latent), BF16)],
        [mine, swap_core(others)],
        [me],
        flops=8 * patch_rep.size,
    )

    def finish(forward, values, partial):
        return call(
            functools.partial(finish_kernel, forward),
            [shape(values.shape, BF16)],
            [patch_lengths, values, partial] + [swap_x(partial, k) for k in (1, 2, 3)],
            flops=4 * patches * values.size,
        )[0]

    byte_out = finish(True, byte_states, decoded)
    return byte_out, finish(False, byte_cot, grad_pool), latent_states


def solution(mesh):
    fine = Mesh(mesh.devices.reshape(4, 4, 2, 4), ("y", "z", "c", "x"))
    return jax.shard_map(
        on_device,
        mesh=fine,
        in_specs=(
            P(SEQ, None),
            P(SEQ, None),
            P(SEQ, None),
            P(None, "x"),
            P("x", SEQ),
            P("x", SEQ),
            P(SEQ, "x"),
            P("x", None),
            P(SEQ, None),
        ),
        out_specs=(P(SEQ, None), P(SEQ, None), P(SEQ, "x")),
        check_vma=False,
    )
```

```python
import functools

import jax
import jax.numpy as jnp
from jax import lax
from jax.experimental import pallas as pl
from jax.experimental.pallas import tpu as pltpu
from jax.sharding import Mesh
from jax.sharding import PartitionSpec as P

F32 = jnp.float32
BF16 = jnp.bfloat16
SEQ = ("y", "z", "c")
VMEM_LIMIT = 16 * 1024 * 1024


def swap_core(value):
    return lax.ppermute(value, "c", [(0, 1), (1, 0)])


def swap_x(value, k):
    return lax.ppermute(value, "x", [(i, i ^ k) for i in range(4)])


def swap_near(value, first):
    steps = (1, 3) if first else (3, 1)
    return lax.ppermute(
        value, ("c", "x"), [(c * 4 + x, c * 4 + (x ^ steps[c])) for c in range(2) for x in range(4)]
    )


def swap_first(value, k, first=True):
    pairs = []
    for index in range(32):
        along_z = (index % 2 == 0) == first
        pairs.append((index, index ^ (2 * k if along_z else 8 * k)))
    return lax.ppermute(value, SEQ, pairs)


def swap_second(value, k):
    return swap_first(value, k, False)


def dot(a, b):
    return jnp.dot(a, b, preferred_element_type=F32)


def dot_t(a, b):
    return lax.dot_general(a, b, (((1,), (1,)), ((), ())), preferred_element_type=F32)


def call(body, outs, inputs, scalars=(), flops=0, scratch=(), outside=False):
    specs = [pl.BlockSpec(memory_space=pltpu.SMEM)] * len(scalars)
    specs += [pl.BlockSpec(memory_space=pltpu.HBM if outside else pltpu.VMEM)] * len(inputs)
    moved = sum(v.size * v.dtype.itemsize for v in list(inputs) + list(outs))
    return pl.pallas_call(
        body,
        out_shape=outs,
        in_specs=specs,
        out_specs=[pl.BlockSpec(memory_space=pltpu.VMEM)] * len(outs),
        scratch_shapes=list(scratch),
        compiler_params=pltpu.CompilerParams(vmem_limit_bytes=60 * 1024 * 1024 if outside else VMEM_LIMIT),
        cost_estimate=pl.CostEstimate(flops=flops, bytes_accessed=moved, transcendentals=0),
    )(*scalars, *inputs)


def shape(dims, dtype):
    return jax.ShapeDtypeStruct(dims, dtype)


def bounds(lengths):
    count = lengths.shape[1]
    row = lax.broadcasted_iota(jnp.int32, (count, count), 0)
    column = lax.broadcasted_iota(jnp.int32, (count, count), 1)
    wide = jnp.broadcast_to(lengths, (count, count)).astype(F32)
    ends = jnp.sum(jnp.where(column <= row, wide, 0.0), axis=1, keepdims=True)
    size = jnp.sum(jnp.where(column == row, wide, 0.0), axis=1, keepdims=True)
    return ends - size, ends, size


def membership(lengths, length):
    starts, ends, size = bounds(lengths)
    count = lengths.shape[1]
    position = lax.broadcasted_iota(jnp.int32, (count, length), 1).astype(F32)
    inside = (position >= starts) & (position < ends)
    return jnp.where(inside, 1.0, 0.0).astype(BF16), size


def pool_kernel(lengths, states, cots, pooled):
    pooling, size = membership(lengths[...], states.shape[0])
    width = states.shape[1]
    pooled[:, :width] = (dot(pooling, states[...]) / size).astype(BF16)
    pooled[:, width:] = dot(pooling, cots[...]).astype(BF16)


def stack_kernel(own, one, two, three, out):
    span = own.shape[0]
    for k, block in enumerate((own, one, two, three)):
        out[k * span : (k + 1) * span] = block[...]


def cut_products(count, offsets, whole, keep, send):
    part = keep.shape[0] // (2 * count)
    for k in range(4):
        out = keep if k < 2 else send
        for i in range(count):
            place = pl.multiple_of(offsets[k] + i * 4 * part, 16)
            to = (k % 2) * count * part + i * part
            out[to : to + part] = whole[pl.ds(place, part), :]


def gate_product_kernel(
    offsets, enc_hbm, gate_hbm, lift_hbm, keep, send, w_enc, w_gate, w_lift, whole, sems
):
    copies = [
        pltpu.make_async_copy(source, target, sems.at[i])
        for i, (source, target) in enumerate(
            ((enc_hbm, w_enc), (gate_hbm, w_gate), (lift_hbm, w_lift))
        )
    ]
    for copy in copies:
        copy.start()
    hid = w_gate.shape[0]
    copies[0].wait()
    copies[1].wait()
    whole[:hid] = dot_t(w_gate[...], w_enc[...]).astype(BF16)
    copies[2].wait()
    whole[hid:] = dot_t(w_lift[...], w_enc[...]).astype(BF16)
    cut_products(2, offsets, whole, keep, send)


def down_product_kernel(offsets, w_down, w_dec, w_enc, pooled, keep, send, rep, back, whole):
    whole[...] = dot(w_down[...], w_dec[...]).astype(BF16)
    cut_products(1, offsets, whole, keep, send)
    width = w_enc.shape[0]
    rep[...] = dot(pooled[:, :width], w_enc[...]).astype(BF16)
    back[...] = dot_t(dot_t(pooled[:, width:], w_dec[...]).astype(BF16), w_enc[...])


def halve_kernel(keep, first, own, send):
    half = own.shape[0]
    own[...] = keep[:half].astype(F32) + first[:half].astype(F32)
    send[...] = (keep[half:].astype(F32) + first[half:].astype(F32)).astype(BF16)


def gate_rows(rows, products):
    width = products.shape[1]
    both = dot_t(products[...], jnp.concatenate([block[:, :width] for block in rows], axis=0))
    part = both.shape[0] // 2
    return both[:part], both[part:]


def hidden_rows(rows, products):
    gate, lift = gate_rows(rows, products)
    return (gate * (1.0 / (1.0 + jnp.exp(-gate))) * lift).astype(BF16)


def near_kernel(r0, r1, r2, r3, own, second, products, hidden):
    products[...] = (own[...] + second[...].astype(F32)).astype(BF16)
    hidden[...] = hidden_rows((r0, r1, r2, r3), products)


def far_kernel(r0, r1, r2, r3, products, near_hidden, hidden):
    half = near_hidden.shape[1]
    hidden[:, :half] = near_hidden[...]
    hidden[:, half:] = hidden_rows((r0, r1, r2, r3), products)


def grad_rows(rows, down, products):
    width = down.shape[1]
    grad_hidden = dot_t(down, jnp.concatenate([block[:, width:] for block in rows], axis=0))
    gate, lift = gate_rows(rows, products)
    sig = 1.0 / (1.0 + jnp.exp(-gate))
    grad_gate = grad_hidden * lift * sig * (1.0 + gate * (1.0 - sig))
    return jnp.concatenate([grad_gate, grad_hidden * (gate * sig)], axis=0).astype(BF16)


def grad_far_kernel(r0, r1, r2, r3, own, second, products, down, partial):
    down[...] = (own[...] + second[...].astype(F32)).astype(BF16)
    grads = grad_rows((r0, r1, r2, r3), down[...], products)
    partial[...] = dot(grads.T, products[...]).astype(BF16)


def place_blocks(total, outs):
    patches = total.shape[0] // 16
    for first, out in enumerate(outs):
        for second in range(4):
            place = (4 * second + first) * patches
            out[second * patches : (second + 1) * patches] = total[place : place + patches].astype(BF16)


def down_far_kernel(offsets, own, one, two, three, w_down, out, stack):
    part, span = own.shape[0], out.shape[0]
    for k, block in enumerate((own, one, two, three)):
        stack[pl.ds(pl.multiple_of(offsets[k], 16), part), :] = block[:, span:]
    out[...] = dot(stack[...].T, w_down[...]).astype(BF16)


def sum_near_kernel(
    offsets, own, one, two, three, w_down, other, r0, r1, r2, r3, down, products, grad_other, *rest
):
    stack = rest[-1]
    part, span = own.shape[0], other.shape[0]
    width = w_down.shape[1]
    for k, block in enumerate((own, one, two, three)):
        stack[pl.ds(pl.multiple_of(offsets[k], 16), part), :] = block[:, :span]
    grads = grad_rows((r0, r1, r2, r3), down[...], products)
    total = dot(grads.T, products[...]) + grad_other[...].astype(F32)
    place_blocks(total, [out.at[:, width:] for out in rest[:-1]])
    total = dot(stack[...].T, w_down[...]) + other[...].astype(F32)
    place_blocks(total, [out.at[:, :width] for out in rest[:-1]])


def add_kernel(own, one, two, three, *outs):
    total = (
        own[...].astype(F32) + one[...].astype(F32) + two[...].astype(F32) + three[...].astype(F32)
    )
    patches = own.shape[0] // 4
    for i, out in enumerate(outs):
        out[...] = total[i * patches : (i + 1) * patches].astype(out.dtype)


def decode_kernel(own, one, two, three, rep, back, weight, owners, partial, outgoing):
    width = rep.shape[1]
    total = own[...] + one[...].astype(F32) + two[...].astype(F32) + three[...].astype(F32)
    states = (total[:, :width] + rep[...].astype(F32)).astype(BF16)
    partial[:, : weight.shape[1]] = dot(states, weight[...]).astype(BF16)
    partial[:, weight.shape[1] :] = (total[:, width:] + back[...]).astype(BF16)
    count = rep.shape[0]
    own_row = jnp.broadcast_to(owners[...], (count, count))
    row = lax.broadcasted_iota(jnp.int32, (count, count), 0)
    column = lax.broadcasted_iota(jnp.int32, (count, count), 1)
    own_column = jnp.sum(jnp.where(row == column, own_row, 0), axis=1, keepdims=True)
    same = jnp.where((own_column == own_row) & (row < column), 1, 0)
    rank = jnp.sum(same, axis=0, keepdims=True)
    targets = 2 * owners[...] + rank
    slots = lax.broadcasted_iota(jnp.int32, (2 * count, count), 0)
    routing = jnp.where(slots == targets, 1.0, 0.0).astype(BF16)
    outgoing[...] = dot(routing, states).astype(BF16)


def finish_kernel(lengths, states, cots, own, one, two, three, out, grad):
    total = (
        own[...].astype(F32) + one[...].astype(F32) + two[...].astype(F32) + three[...].astype(F32)
    )
    pooling, size = membership(lengths[...], states.shape[0])
    width = states.shape[1]
    pick = (((0,), (0,)), ((), ()))
    for values, result, part in (
        (states, out, total[:, :width]),
        (cots, grad, total[:, width:] / size),
    ):
        high = part.astype(BF16)
        low = (part - high.astype(F32)).astype(BF16)
        spread = lax.dot_general(pooling, high, pick, preferred_element_type=F32)
        spread = spread + lax.dot_general(pooling, low, pick, preferred_element_type=F32)
        result[...] = (values[...].astype(F32) + spread).astype(BF16)


def on_device(
    byte_states, patch_lengths, patch_owner, w_enc, w_gate, w_lift, w_down, w_dec, byte_cot
):
    patches = patch_lengths.shape[1]
    width = byte_states.shape[1]
    latent = w_enc.shape[1]
    hid = w_gate.shape[1]
    part = hid // 4
    group = 16 * patches
    x, core = lax.axis_index("x"), lax.axis_index("c")
    step = jnp.where(core == 0, 1, 3)
    halving = (jnp.stack([x, x ^ step ^ 2, x ^ step, x ^ 2]) * part).astype(jnp.int32)
    offsets = (jnp.stack([x, x ^ 1, x ^ 2, x ^ 3]) * part).astype(jnp.int32)
    owners = patch_owner.reshape(1, patches)
    w_gate, w_lift = w_gate.T, w_lift.T

    def after(value, token):
        return lax.optimization_barrier((value, token))[0]

    def over(swap, own, *sends):
        sends = sends or (own,) * 3
        two, one, three = [swap(sends[k - 1], k) for k in (2, 1, 3)]
        return [own, one, two, three]

    def halve(keep, first):
        own, send = call(
            halve_kernel,
            [shape((keep.shape[0] // 2, width), F32), shape((keep.shape[0] // 2, width), BF16)],
            [keep, first],
            flops=2 * keep.size,
        )
        return own, swap_near(send, False)

    weights = [w_enc, w_gate, w_lift]
    keep, send = call(
        gate_product_kernel,
        [shape((4 * part, width), BF16)] * 2,
        weights,
        [halving],
        flops=4 * hid * width * latent,
        scratch=[pltpu.VMEM(w.shape, BF16) for w in weights]
        + [pltpu.VMEM((2 * hid, width), BF16), pltpu.SemaphoreType.DMA((3,))],
        outside=True,
    )
    first = swap_near(send, True)
    (pooled,) = call(
        pool_kernel,
        [shape((patches, 2 * width), BF16)],
        [patch_lengths, after(byte_states, send), byte_cot],
        flops=4 * patches * byte_states.size,
    )
    (rows,) = call(
        stack_kernel,
        [shape((4 * patches, 2 * width), BF16)],
        over(swap_first, pooled),
        flops=8 * patches * width,
    )
    near = over(swap_second, rows)
    far = [swap_core(block) for block in near]
    down_keep, down_send, patch_rep, back = call(
        down_product_kernel,
        [shape((2 * part, width), BF16)] * 2
        + [shape((patches, latent), BF16), shape((patches, width), F32)],
        [w_down, w_dec, w_enc, pooled],
        [halving],
        flops=2 * hid * width * latent,
        scratch=[pltpu.VMEM((hid, width), BF16)],
    )
    own, second = halve(keep, first)
    down_first = swap_near(after(down_send, first), True)
    flops = 4 * group * width * part
    products, near_hidden = call(
        near_kernel,
        [
            shape((2 * part, width), BF16),
            shape((part, group), BF16),
        ],
        [*near, after(own, down_send), second],
        flops=flops,
    )
    (hidden,) = call(
        far_kernel,
        [shape((part, 2 * group), BF16)],
        [*far, products, near_hidden],
        flops=flops,
    )
    hiddens = over(swap_x, hidden)
    down_own, down_second = halve(down_keep, down_first)
    down, far_partial = call(
        grad_far_kernel,
        [shape((part, width), BF16), shape((group, width), BF16)],
        [*far, down_own, down_second, products],
        flops=flops,
    )
    (far_rows,) = call(
        down_far_kernel,
        [shape((group, latent), BF16)],
        [*hiddens, w_down],
        [offsets],
        flops=2 * group * latent * hid,
        scratch=[pltpu.VMEM((hid, group), BF16)],
    )
    terms = call(
        sum_near_kernel,
        [shape((4 * patches, latent + width), BF16)] * 4,
        [
            *hiddens,
            w_down,
            swap_core(far_rows),
            *near,
            down,
            products,
            swap_core(far_partial),
        ],
        [offsets],
        flops=2 * group * latent * hid + flops,
        scratch=[pltpu.VMEM((hid, group), BF16)],
    )
    own, *sends = call(
        add_kernel,
        [shape((patches, latent + width), F32)] + [shape((patches, latent + width), BF16)] * 3,
        over(swap_first, *terms),
        flops=32 * patches * width,
    )
    partial, outgoing = call(
        decode_kernel,
        [shape((patches, 2 * width), BF16), shape((2 * patches, latent), BF16)],
        [*over(swap_second, own, *sends), patch_rep, back, w_dec, owners],
        flops=2 * patches * width * latent,
    )
    latent_states = lax.all_to_all(outgoing, SEQ, split_axis=0, concat_axis=0, tiled=True)
    partials = over(swap_x, partial)
    byte_out, byte_grad = call(
        finish_kernel,
        [shape(byte_states.shape, BF16), shape(byte_cot.shape, BF16)],
        [patch_lengths, byte_states, byte_cot, *partials],
        flops=16 * patches * byte_states.size,
    )
    return byte_out, byte_grad, latent_states


def solution(mesh):
    fine = Mesh(mesh.devices.reshape(4, 4, 2, 4), ("y", "z", "c", "x"))
    return jax.shard_map(
        on_device,
        mesh=fine,
        in_specs=(
            P(SEQ, None),
            P(SEQ, None),
            P(SEQ, None),
            P(None, "x"),
            P("x", SEQ),
            P("x", SEQ),
            P(SEQ, "x"),
            P("x", None),
            P(SEQ, None),
        ),
        out_specs=(P(SEQ, None), P(SEQ, None), P(SEQ, "x")),
        check_vma=False,
    )
```

```python
import functools

import jax
import jax.numpy as jnp
from jax import lax
from jax.experimental import pallas as pl
from jax.experimental.pallas import tpu as pltpu
from jax.sharding import Mesh
from jax.sharding import PartitionSpec as P

F32 = jnp.float32
BF16 = jnp.bfloat16
SEQ = ("y", "z", "c")
VMEM_LIMIT = 32 * 1024 * 1024


def swap_core(value):
    return lax.ppermute(value, "c", [(0, 1), (1, 0)])


def swap_x(value, k):
    return lax.ppermute(value, "x", [(i, i ^ k) for i in range(4)])


def swap_near(value, first):
    steps = (1, 3) if first else (3, 1)
    return lax.ppermute(
        value, ("c", "x"), [(c * 4 + x, c * 4 + (x ^ steps[c])) for c in range(2) for x in range(4)]
    )


def swap_first(value, k, first=True):
    pairs = []
    for index in range(32):
        along_z = (index % 2 == 0) == first
        pairs.append((index, index ^ (2 * k if along_z else 8 * k)))
    return lax.ppermute(value, SEQ, pairs)


def swap_second(value, k):
    return swap_first(value, k, False)


def dot(a, b):
    return jnp.dot(a, b, preferred_element_type=F32)


def dot_t(a, b):
    return lax.dot_general(a, b, (((1,), (1,)), ((), ())), preferred_element_type=F32)


def call(body, outs, inputs, scalars=(), flops=0, scratch=(), outside=False):
    specs = [pl.BlockSpec(memory_space=pltpu.SMEM)] * len(scalars)
    specs += [pl.BlockSpec(memory_space=pltpu.HBM if outside else pltpu.VMEM)] * len(inputs)
    moved = sum(v.size * v.dtype.itemsize for v in list(inputs) + list(outs))
    return pl.pallas_call(
        body,
        out_shape=outs,
        in_specs=specs,
        out_specs=[pl.BlockSpec(memory_space=pltpu.VMEM)] * len(outs),
        scratch_shapes=list(scratch),
        compiler_params=pltpu.CompilerParams(vmem_limit_bytes=60 * 1024 * 1024 if outside else VMEM_LIMIT),
        cost_estimate=pl.CostEstimate(flops=flops, bytes_accessed=moved, transcendentals=0),
    )(*scalars, *inputs)


def shape(dims, dtype):
    return jax.ShapeDtypeStruct(dims, dtype)


def bounds(lengths):
    count = lengths.shape[1]
    row = lax.broadcasted_iota(jnp.int32, (count, count), 0)
    column = lax.broadcasted_iota(jnp.int32, (count, count), 1)
    wide = jnp.broadcast_to(lengths, (count, count)).astype(F32)
    ends = jnp.sum(jnp.where(column <= row, wide, 0.0), axis=1, keepdims=True)
    size = jnp.sum(jnp.where(column == row, wide, 0.0), axis=1, keepdims=True)
    return ends - size, ends, size


def membership(lengths, length):
    starts, ends, size = bounds(lengths)
    count = lengths.shape[1]
    position = lax.broadcasted_iota(jnp.int32, (count, length), 1).astype(F32)
    inside = (position >= starts) & (position < ends)
    return jnp.where(inside, 1.0, 0.0).astype(BF16), size


def pool_kernel(lengths, states, cots, pooled):
    pooling, size = membership(lengths[...], states.shape[0])
    width = states.shape[1]
    pooled[:, :width] = (dot(pooling, states[...]) / size).astype(BF16)
    pooled[:, width:] = dot(pooling, cots[...]).astype(BF16)


def stack_kernel(own, one, two, three, out):
    span = own.shape[0]
    for k, block in enumerate((own, one, two, three)):
        out[k * span : (k + 1) * span] = block[...]


def cut_products(count, offsets, whole, keep, send):
    part = keep.shape[0] // (2 * count)
    for k in range(4):
        out = keep if k < 2 else send
        for i in range(count):
            place = pl.multiple_of(offsets[k] + i * 4 * part, 16)
            to = (k % 2) * count * part + i * part
            out[to : to + part] = whole[pl.ds(place, part), :]


def product_kernel(offsets, *refs):
    sources, (keep, send), (w_enc, w_gate, w_lift, w_down, w_dec, whole, sems) = (
        refs[:5],
        refs[5:7],
        refs[7:],
    )
    targets = (w_enc, w_gate, w_lift, w_down, w_dec)
    copies = [
        pltpu.make_async_copy(source, target, sems.at[i])
        for i, (source, target) in enumerate(zip(sources, targets))
    ]
    for copy in copies:
        copy.start()
    hid = w_gate.shape[0]
    copies[0].wait()
    copies[1].wait()
    whole[:hid] = dot_t(w_gate[...], w_enc[...]).astype(BF16)
    copies[2].wait()
    whole[hid : 2 * hid] = dot_t(w_lift[...], w_enc[...]).astype(BF16)
    copies[3].wait()
    copies[4].wait()
    whole[2 * hid :] = dot(w_down[...], w_dec[...]).astype(BF16)
    cut_products(3, offsets, whole, keep, send)


def encode_kernel(w_dec, w_enc, pooled, rep, back):
    width = w_enc.shape[0]
    rep[...] = dot(pooled[:, :width], w_enc[...]).astype(BF16)
    back[...] = dot_t(dot_t(pooled[:, width:], w_dec[...]).astype(BF16), w_enc[...])


def halve_kernel(keep, first, own, send):
    half = own.shape[0]
    own[...] = keep[:half].astype(F32) + first[:half].astype(F32)
    send[...] = (keep[half:].astype(F32) + first[half:].astype(F32)).astype(BF16)


def gate_rows(rows, products):
    width = products.shape[1]
    part = products.shape[0] // 3
    both = dot_t(products[: 2 * part], jnp.concatenate([block[:, :width] for block in rows], axis=0))
    return both[:part], both[part:]


def hidden_rows(rows, products):
    gate, lift = gate_rows(rows, products)
    return (gate * (1.0 / (1.0 + jnp.exp(-gate))) * lift).astype(BF16)


def near_kernel(r0, r1, r2, r3, own, second, products, hidden):
    products[...] = (own[...] + second[...].astype(F32)).astype(BF16)
    hidden[...] = hidden_rows((r0, r1, r2, r3), products)


def far_kernel(r0, r1, r2, r3, products, near_hidden, hidden):
    half = near_hidden.shape[1]
    hidden[:, :half] = near_hidden[...]
    hidden[:, half:] = hidden_rows((r0, r1, r2, r3), products)


def grad_rows(rows, products):
    width = products.shape[1]
    part = products.shape[0] // 3
    grad_hidden = dot_t(
        products[2 * part :], jnp.concatenate([block[:, width:] for block in rows], axis=0)
    )
    gate, lift = gate_rows(rows, products)
    sig = 1.0 / (1.0 + jnp.exp(-gate))
    grad_gate = grad_hidden * lift * sig * (1.0 + gate * (1.0 - sig))
    grads = jnp.concatenate([grad_gate, grad_hidden * (gate * sig)], axis=0).astype(BF16)
    return dot(grads.T, products[: 2 * part])


def grad_far_kernel(r0, r1, r2, r3, products, partial):
    partial[...] = grad_rows((r0, r1, r2, r3), products).astype(BF16)


def place_blocks(total, outs):
    patches = total.shape[0] // 16
    for first, out in enumerate(outs):
        for second in range(4):
            place = (4 * second + first) * patches
            out[second * patches : (second + 1) * patches] = total[place : place + patches].astype(BF16)


def down_far_kernel(offsets, own, one, two, three, w_down, out, stack):
    part, span = own.shape[0], out.shape[0]
    for k, block in enumerate((own, one, two, three)):
        stack[pl.ds(pl.multiple_of(offsets[k], 16), part), :] = block[:, span:]
    out[...] = dot(stack[...].T, w_down[...]).astype(BF16)


def sum_near_kernel(
    offsets, own, one, two, three, w_down, other, r0, r1, r2, r3, products, grad_other, *rest
):
    stack = rest[-1]
    part, span = own.shape[0], other.shape[0]
    width = w_down.shape[1]
    for k, block in enumerate((own, one, two, three)):
        stack[pl.ds(pl.multiple_of(offsets[k], 16), part), :] = block[:, :span]
    total = grad_rows((r0, r1, r2, r3), products) + grad_other[...].astype(F32)
    place_blocks(total, [out.at[:, width:] for out in rest[:-1]])
    total = dot(stack[...].T, w_down[...]) + other[...].astype(F32)
    place_blocks(total, [out.at[:, :width] for out in rest[:-1]])


def add_kernel(own, one, two, three, *outs):
    total = (
        own[...].astype(F32) + one[...].astype(F32) + two[...].astype(F32) + three[...].astype(F32)
    )
    patches = own.shape[0] // 4
    for i, out in enumerate(outs):
        out[...] = total[i * patches : (i + 1) * patches].astype(out.dtype)


def decode_kernel(own, one, two, three, rep, back, weight, owners, partial, outgoing):
    width = rep.shape[1]
    total = own[...] + one[...].astype(F32) + two[...].astype(F32) + three[...].astype(F32)
    states = (total[:, :width] + rep[...].astype(F32)).astype(BF16)
    partial[:, : weight.shape[1]] = dot(states, weight[...]).astype(BF16)
    partial[:, weight.shape[1] :] = (total[:, width:] + back[...]).astype(BF16)
    count = rep.shape[0]
    own_row = jnp.broadcast_to(owners[...], (count, count))
    row = lax.broadcasted_iota(jnp.int32, (count, count), 0)
    column = lax.broadcasted_iota(jnp.int32, (count, count), 1)
    own_column = jnp.sum(jnp.where(row == column, own_row, 0), axis=1, keepdims=True)
    same = jnp.where((own_column == own_row) & (row < column), 1, 0)
    rank = jnp.sum(same, axis=0, keepdims=True)
    targets = 2 * owners[...] + rank
    slots = lax.broadcasted_iota(jnp.int32, (2 * count, count), 0)
    routing = jnp.where(slots == targets, 1.0, 0.0).astype(BF16)
    outgoing[...] = dot(routing, states).astype(BF16)


def finish_kernel(lengths, states, cots, own, one, two, three, out, grad):
    total = (
        own[...].astype(F32) + one[...].astype(F32) + two[...].astype(F32) + three[...].astype(F32)
    )
    pooling, size = membership(lengths[...], states.shape[0])
    width = states.shape[1]
    pick = (((0,), (0,)), ((), ()))
    for values, result, part in (
        (states, out, total[:, :width]),
        (cots, grad, total[:, width:] / size),
    ):
        high = part.astype(BF16)
        low = (part - high.astype(F32)).astype(BF16)
        spread = lax.dot_general(pooling, high, pick, preferred_element_type=F32)
        spread = spread + lax.dot_general(pooling, low, pick, preferred_element_type=F32)
        result[...] = (values[...].astype(F32) + spread).astype(BF16)


def on_device(
    byte_states, patch_lengths, patch_owner, w_enc, w_gate, w_lift, w_down, w_dec, byte_cot
):
    patches = patch_lengths.shape[1]
    width = byte_states.shape[1]
    latent = w_enc.shape[1]
    hid = w_gate.shape[1]
    part = hid // 4
    group = 16 * patches
    x, core = lax.axis_index("x"), lax.axis_index("c")
    step = jnp.where(core == 0, 1, 3)
    halving = (jnp.stack([x, x ^ step ^ 2, x ^ step, x ^ 2]) * part).astype(jnp.int32)
    offsets = (jnp.stack([x, x ^ 1, x ^ 2, x ^ 3]) * part).astype(jnp.int32)
    owners = patch_owner.reshape(1, patches)
    w_gate, w_lift = w_gate.T, w_lift.T

    def after(value, token):
        return lax.optimization_barrier((value, token))[0]

    def over(swap, own, *sends):
        sends = sends or (own,) * 3
        two, one, three = [swap(sends[k - 1], k) for k in (2, 1, 3)]
        return [own, one, two, three]

    def halve(keep, first):
        own, send = call(
            halve_kernel,
            [shape((keep.shape[0] // 2, width), F32), shape((keep.shape[0] // 2, width), BF16)],
            [keep, first],
            flops=2 * keep.size,
        )
        return own, swap_near(send, False)

    weights = [w_enc, w_gate, w_lift, w_down, w_dec]
    keep, send = call(
        product_kernel,
        [shape((6 * part, width), BF16)] * 2,
        weights,
        [halving],
        flops=6 * hid * width * latent,
        scratch=[pltpu.VMEM(w.shape, BF16) for w in weights]
        + [pltpu.VMEM((3 * hid, width), BF16), pltpu.SemaphoreType.DMA((5,))],
        outside=True,
    )
    first = swap_near(send, True)
    (pooled,) = call(
        pool_kernel,
        [shape((patches, 2 * width), BF16)],
        [patch_lengths, after(byte_states, send), byte_cot],
        flops=4 * patches * byte_states.size,
    )
    (rows,) = call(
        stack_kernel,
        [shape((4 * patches, 2 * width), BF16)],
        over(swap_first, pooled),
        flops=8 * patches * width,
    )
    near = over(swap_second, rows)
    far = [swap_core(block) for block in near]
    own, second = halve(keep, first)
    flops = 4 * group * width * part
    products, near_hidden = call(
        near_kernel,
        [
            shape((3 * part, width), BF16),
            shape((part, group), BF16),
        ],
        [*near, own, second],
        flops=flops,
    )
    (hidden,) = call(
        far_kernel,
        [shape((part, 2 * group), BF16)],
        [*far, products, near_hidden],
        flops=flops,
    )
    hiddens = over(swap_x, hidden)
    (far_partial,) = call(
        grad_far_kernel,
        [shape((group, width), BF16)],
        [*far, products],
        flops=flops,
    )
    patch_rep, back = call(
        encode_kernel,
        [shape((patches, latent), BF16), shape((patches, width), F32)],
        [w_dec, w_enc, pooled],
        flops=6 * patches * width * latent,
    )
    (far_rows,) = call(
        down_far_kernel,
        [shape((group, latent), BF16)],
        [*hiddens, after(w_down, (far_partial, back))],
        [offsets],
        flops=2 * group * latent * hid,
        scratch=[pltpu.VMEM((hid, group), BF16)],
    )
    terms = call(
        sum_near_kernel,
        [shape((4 * patches, latent + width), BF16)] * 4,
        [
            *hiddens,
            w_down,
            swap_core(far_rows),
            *near,
            products,
            swap_core(far_partial),
        ],
        [offsets],
        flops=2 * group * latent * hid + flops,
        scratch=[pltpu.VMEM((hid, group), BF16)],
    )
    own, *sends = call(
        add_kernel,
        [shape((patches, latent + width), F32)] + [shape((patches, latent + width), BF16)] * 3,
        over(swap_first, *terms),
        flops=32 * patches * width,
    )
    partial, outgoing = call(
        decode_kernel,
        [shape((patches, 2 * width), BF16), shape((2 * patches, latent), BF16)],
        [*over(swap_second, own, *sends), patch_rep, back, w_dec, owners],
        flops=2 * patches * width * latent,
    )
    latent_states = lax.all_to_all(outgoing, SEQ, split_axis=0, concat_axis=0, tiled=True)
    partials = over(swap_x, partial)
    byte_out, byte_grad = call(
        finish_kernel,
        [shape(byte_states.shape, BF16), shape(byte_cot.shape, BF16)],
        [patch_lengths, byte_states, byte_cot, *partials],
        flops=16 * patches * byte_states.size,
    )
    return byte_out, byte_grad, latent_states


def solution(mesh):
    fine = Mesh(mesh.devices.reshape(4, 4, 2, 4), ("y", "z", "c", "x"))
    return jax.shard_map(
        on_device,
        mesh=fine,
        in_specs=(
            P(SEQ, None),
            P(SEQ, None),
            P(SEQ, None),
            P(None, "x"),
            P("x", SEQ),
            P("x", SEQ),
            P(SEQ, "x"),
            P("x", None),
            P(SEQ, None),
        ),
        out_specs=(P(SEQ, None), P(SEQ, None), P(SEQ, "x")),
        check_vma=False,
    )
```

```python
import functools

import jax
import jax.numpy as jnp
from jax import lax
from jax.experimental import pallas as pl
from jax.experimental.pallas import tpu as pltpu
from jax.sharding import Mesh
from jax.sharding import PartitionSpec as P

F32 = jnp.float32
BF16 = jnp.bfloat16
SEQ = ("y", "z", "c")
VMEM_LIMIT = 32 * 1024 * 1024


def swap_core(value):
    return lax.ppermute(value, "c", [(0, 1), (1, 0)])


def swap_x(value, k):
    return lax.ppermute(value, "x", [(i, i ^ k) for i in range(4)])


def swap_near(value, first):
    steps = (1, 3) if first else (3, 1)
    return lax.ppermute(
        value, ("c", "x"), [(c * 4 + x, c * 4 + (x ^ steps[c])) for c in range(2) for x in range(4)]
    )


def swap_first(value, k, first=True):
    pairs = []
    for index in range(32):
        along_z = (index % 2 == 0) == first
        pairs.append((index, index ^ (2 * k if along_z else 8 * k)))
    return lax.ppermute(value, SEQ, pairs)


def swap_second(value, k):
    return swap_first(value, k, False)


def dot(a, b):
    return jnp.dot(a, b, preferred_element_type=F32)


def dot_t(a, b):
    return lax.dot_general(a, b, (((1,), (1,)), ((), ())), preferred_element_type=F32)


def call(body, outs, inputs, scalars=(), flops=0, scratch=(), outside=False):
    specs = [pl.BlockSpec(memory_space=pltpu.SMEM)] * len(scalars)
    specs += [pl.BlockSpec(memory_space=pltpu.HBM if outside else pltpu.VMEM)] * len(inputs)
    moved = sum(v.size * v.dtype.itemsize for v in list(inputs) + list(outs))
    return pl.pallas_call(
        body,
        out_shape=outs,
        in_specs=specs,
        out_specs=[pl.BlockSpec(memory_space=pltpu.VMEM)] * len(outs),
        scratch_shapes=list(scratch),
        compiler_params=pltpu.CompilerParams(vmem_limit_bytes=60 * 1024 * 1024 if outside else VMEM_LIMIT),
        cost_estimate=pl.CostEstimate(flops=flops, bytes_accessed=moved, transcendentals=0),
    )(*scalars, *inputs)


def shape(dims, dtype):
    return jax.ShapeDtypeStruct(dims, dtype)


def bounds(lengths):
    count = lengths.shape[1]
    row = lax.broadcasted_iota(jnp.int32, (count, count), 0)
    column = lax.broadcasted_iota(jnp.int32, (count, count), 1)
    wide = jnp.broadcast_to(lengths, (count, count)).astype(F32)
    ends = jnp.sum(jnp.where(column <= row, wide, 0.0), axis=1, keepdims=True)
    size = jnp.sum(jnp.where(column == row, wide, 0.0), axis=1, keepdims=True)
    return ends - size, ends, size


def membership(lengths, length):
    starts, ends, size = bounds(lengths)
    count = lengths.shape[1]
    position = lax.broadcasted_iota(jnp.int32, (count, length), 1).astype(F32)
    inside = (position >= starts) & (position < ends)
    return jnp.where(inside, 1.0, 0.0).astype(BF16), size


def pool_kernel(lengths, states, cots, pooled):
    pooling, size = membership(lengths[...], states.shape[0])
    width = states.shape[1]
    pooled[:, :width] = (dot(pooling, states[...]) / size).astype(BF16)
    pooled[:, width:] = dot(pooling, cots[...]).astype(BF16)


def stack_kernel(own, one, two, three, out):
    span = own.shape[0]
    for k, block in enumerate((own, one, two, three)):
        out[k * span : (k + 1) * span] = block[...]


def cut_products(count, offsets, whole, keep, send):
    part = keep.shape[0] // (2 * count)
    for k in range(4):
        out = keep if k < 2 else send
        for i in range(count):
            place = pl.multiple_of(offsets[k] + i * 4 * part, 16)
            to = (k % 2) * count * part + i * part
            out[to : to + part] = whole[pl.ds(place, part), :]


def product_kernel(offsets, *refs):
    sources, (keep, send), (w_enc, w_gate, w_lift, w_down, w_dec, whole, sems) = (
        refs[:5],
        refs[5:7],
        refs[7:],
    )
    targets = (w_enc, w_gate, w_lift, w_down, w_dec)
    copies = [
        pltpu.make_async_copy(source, target, sems.at[i])
        for i, (source, target) in enumerate(zip(sources, targets))
    ]
    for copy in copies:
        copy.start()
    hid = w_gate.shape[0]
    copies[0].wait()
    copies[1].wait()
    whole[:hid] = dot_t(w_gate[...], w_enc[...]).astype(BF16)
    copies[2].wait()
    whole[hid : 2 * hid] = dot_t(w_lift[...], w_enc[...]).astype(BF16)
    copies[3].wait()
    copies[4].wait()
    whole[2 * hid :] = dot(w_down[...], w_dec[...]).astype(BF16)
    cut_products(3, offsets, whole, keep, send)


def encode_kernel(w_dec, w_enc, pooled, rep, back):
    width = w_enc.shape[0]
    rep[...] = dot(pooled[:, :width], w_enc[...]).astype(BF16)
    back[...] = dot_t(dot_t(pooled[:, width:], w_dec[...]).astype(BF16), w_enc[...])


def halve_kernel(keep, first, own, send):
    half = own.shape[0]
    own[...] = keep[:half].astype(F32) + first[:half].astype(F32)
    send[...] = (keep[half:].astype(F32) + first[half:].astype(F32)).astype(BF16)


def hidden_rows(rows, products):
    width = products.shape[1]
    part = products.shape[0] // 3
    stacked = [block[...] for block in rows]
    stacked = jnp.concatenate(stacked, axis=0)
    both = dot_t(products[: 2 * part], stacked[:, :width])
    grad_hidden = dot_t(products[2 * part :], stacked[:, width:])
    gate, lift = both[:part], both[part:]
    sig = 1.0 / (1.0 + jnp.exp(-gate))
    silu = gate * sig
    grad_gate = grad_hidden * lift * sig * (1.0 + gate * (1.0 - sig))
    grads = jnp.concatenate([grad_gate, grad_hidden * silu], axis=0).astype(BF16)
    return (silu * lift).astype(BF16), dot(grads.T, products[: 2 * part])


def near_kernel(r0, r1, r2, r3, own, second, products, hidden, partial):
    products[...] = (own[...] + second[...].astype(F32)).astype(BF16)
    hidden[...], partial[...] = hidden_rows((r0, r1, r2, r3), products)


def far_kernel(r0, r1, r2, r3, products, near_hidden, hidden, partial):
    half = near_hidden.shape[1]
    hidden[:, :half] = near_hidden[...]
    hidden[:, half:], terms = hidden_rows((r0, r1, r2, r3), products)
    partial[...] = terms.astype(BF16)


def place_blocks(total, outs):
    patches = total.shape[0] // 16
    for first, out in enumerate(outs):
        for second in range(4):
            place = (4 * second + first) * patches
            out[second * patches : (second + 1) * patches] = total[place : place + patches].astype(BF16)


def down_far_kernel(offsets, own, one, two, three, w_down, out, stack):
    part, span = own.shape[0], out.shape[0]
    for k, block in enumerate((own, one, two, three)):
        stack[pl.ds(pl.multiple_of(offsets[k], 16), part), :] = block[:, span:]
    out[...] = dot(stack[...].T, w_down[...]).astype(BF16)


def grad_near_kernel(partial, other, *outs):
    place_blocks(partial[...] + other[...].astype(F32), outs)


def down_near_kernel(offsets, own, one, two, three, w_down, other, *rest):
    stack = rest[-1]
    part, span = own.shape[0], other.shape[0]
    for k, block in enumerate((own, one, two, three)):
        stack[pl.ds(pl.multiple_of(offsets[k], 16), part), :] = block[:, :span]
    place_blocks(dot(stack[...].T, w_down[...]) + other[...].astype(F32), rest[:-1])


def add_kernel(*refs):
    terms, outs = refs[:8], refs[8:]
    patches, width = terms[0].shape[0] // 4, terms[0].shape[1]
    for i in range(2):
        total = sum(term[...].astype(F32) for term in terms[4 * i : 4 * i + 4])
        for k, out in enumerate(outs):
            rows = total[k * patches : (k + 1) * patches]
            out[:, i * width : (i + 1) * width] = rows.astype(out.dtype)


def decode_kernel(own, one, two, three, rep, back, weight, owners, partial, outgoing):
    width = rep.shape[1]
    total = own[...] + one[...].astype(F32) + two[...].astype(F32) + three[...].astype(F32)
    states = (total[:, :width] + rep[...].astype(F32)).astype(BF16)
    partial[:, : weight.shape[1]] = dot(states, weight[...]).astype(BF16)
    partial[:, weight.shape[1] :] = (total[:, width:] + back[...]).astype(BF16)
    count = rep.shape[0]
    own_row = jnp.broadcast_to(owners[...], (count, count))
    row = lax.broadcasted_iota(jnp.int32, (count, count), 0)
    column = lax.broadcasted_iota(jnp.int32, (count, count), 1)
    own_column = jnp.sum(jnp.where(row == column, own_row, 0), axis=1, keepdims=True)
    same = jnp.where((own_column == own_row) & (row < column), 1, 0)
    rank = jnp.sum(same, axis=0, keepdims=True)
    targets = 2 * owners[...] + rank
    slots = lax.broadcasted_iota(jnp.int32, (2 * count, count), 0)
    routing = jnp.where(slots == targets, 1.0, 0.0).astype(BF16)
    outgoing[...] = dot(routing, states).astype(BF16)


def finish_kernel(lengths, states, cots, own, one, two, three, out, grad):
    total = (
        own[...].astype(F32) + one[...].astype(F32) + two[...].astype(F32) + three[...].astype(F32)
    )
    pooling, size = membership(lengths[...], states.shape[0])
    width = states.shape[1]
    pick = (((0,), (0,)), ((), ()))
    for values, result, part in (
        (states, out, total[:, :width]),
        (cots, grad, total[:, width:] / size),
    ):
        high = part.astype(BF16)
        low = (part - high.astype(F32)).astype(BF16)
        spread = lax.dot_general(pooling, high, pick, preferred_element_type=F32)
        spread = spread + lax.dot_general(pooling, low, pick, preferred_element_type=F32)
        result[...] = (values[...].astype(F32) + spread).astype(BF16)


def on_device(
    byte_states, patch_lengths, patch_owner, w_enc, w_gate, w_lift, w_down, w_dec, byte_cot
):
    patches = patch_lengths.shape[1]
    width = byte_states.shape[1]
    latent = w_enc.shape[1]
    hid = w_gate.shape[1]
    part = hid // 4
    group = 16 * patches
    x, core = lax.axis_index("x"), lax.axis_index("c")
    step = jnp.where(core == 0, 1, 3)
    halving = (jnp.stack([x, x ^ step ^ 2, x ^ step, x ^ 2]) * part).astype(jnp.int32)
    offsets = (jnp.stack([x, x ^ 1, x ^ 2, x ^ 3]) * part).astype(jnp.int32)
    owners = patch_owner.reshape(1, patches)
    w_gate, w_lift = w_gate.T, w_lift.T

    def after(value, token):
        return lax.optimization_barrier((value, token))[0]

    def over(swap, own, *sends):
        sends = sends or (own,) * 3
        two, one, three = [swap(sends[k - 1], k) for k in (2, 1, 3)]
        return [own, one, two, three]

    def halve(keep, first):
        own, send = call(
            halve_kernel,
            [shape((keep.shape[0] // 2, width), F32), shape((keep.shape[0] // 2, width), BF16)],
            [keep, first],
            flops=2 * keep.size,
        )
        return own, swap_near(send, False)

    weights = [w_enc, w_gate, w_lift, w_down, w_dec]
    keep, send = call(
        product_kernel,
        [shape((6 * part, width), BF16)] * 2,
        weights,
        [halving],
        flops=6 * hid * width * latent,
        scratch=[pltpu.VMEM(w.shape, BF16) for w in weights]
        + [pltpu.VMEM((3 * hid, width), BF16), pltpu.SemaphoreType.DMA((5,))],
        outside=True,
    )
    first = swap_near(send, True)
    (pooled,) = call(
        pool_kernel,
        [shape((patches, 2 * width), BF16)],
        [patch_lengths, after(byte_states, send), byte_cot],
        flops=4 * patches * byte_states.size,
    )
    (rows,) = call(
        stack_kernel,
        [shape((4 * patches, 2 * width), BF16)],
        over(swap_first, pooled),
        flops=8 * patches * width,
    )
    near = over(swap_second, rows)
    far = [swap_core(block) for block in near]
    own, second = halve(keep, first)
    flops = 4 * group * width * part
    products, near_hidden, near_partial = call(
        near_kernel,
        [
            shape((3 * part, width), BF16),
            shape((part, group), BF16),
            shape((group, width), F32),
        ],
        [*near, own, second],
        flops=3 * flops,
    )
    hidden, far_partial = call(
        far_kernel,
        [shape((part, 2 * group), BF16), shape((group, width), BF16)],
        [*far, products, near_hidden],
        flops=3 * flops,
    )
    hiddens = over(swap_x, hidden)
    grad_terms = call(
        grad_near_kernel,
        [shape((4 * patches, width), BF16)] * 4,
        [near_partial, swap_core(far_partial)],
        flops=near_partial.size,
    )
    grad_first = over(swap_first, *grad_terms)
    patch_rep, back = call(
        encode_kernel,
        [shape((patches, latent), BF16), shape((patches, width), F32)],
        [w_dec, w_enc, pooled],
        flops=6 * patches * width * latent,
    )
    (far_rows,) = call(
        down_far_kernel,
        [shape((group, latent), BF16)],
        [*hiddens, after(w_down, (*grad_terms, back))],
        [offsets],
        flops=2 * group * latent * hid,
        scratch=[pltpu.VMEM((hid, group), BF16)],
    )
    terms = call(
        down_near_kernel,
        [shape((4 * patches, latent), BF16)] * 4,
        [*hiddens, w_down, swap_core(far_rows)],
        [offsets],
        flops=2 * group * latent * hid,
        scratch=[pltpu.VMEM((hid, group), BF16)],
    )
    own, *sends = call(
        add_kernel,
        [shape((patches, latent + width), F32)] + [shape((patches, latent + width), BF16)] * 3,
        over(swap_first, *terms) + grad_first,
        flops=32 * patches * width,
    )
    partial, outgoing = call(
        decode_kernel,
        [shape((patches, 2 * width), BF16), shape((2 * patches, latent), BF16)],
        [*over(swap_second, own, *sends), patch_rep, back, w_dec, owners],
        flops=2 * patches * width * latent,
    )
    latent_states = lax.all_to_all(outgoing, SEQ, split_axis=0, concat_axis=0, tiled=True)
    partials = over(swap_x, partial)
    byte_out, byte_grad = call(
        finish_kernel,
        [shape(byte_states.shape, BF16), shape(byte_cot.shape, BF16)],
        [patch_lengths, byte_states, byte_cot, *partials],
        flops=16 * patches * byte_states.size,
    )
    return byte_out, byte_grad, latent_states


def solution(mesh):
    fine = Mesh(mesh.devices.reshape(4, 4, 2, 4), ("y", "z", "c", "x"))
    return jax.shard_map(
        on_device,
        mesh=fine,
        in_specs=(
            P(SEQ, None),
            P(SEQ, None),
            P(SEQ, None),
            P(None, "x"),
            P("x", SEQ),
            P("x", SEQ),
            P(SEQ, "x"),
            P("x", None),
            P(SEQ, None),
        ),
        out_specs=(P(SEQ, None), P(SEQ, None), P(SEQ, "x")),
        check_vma=False,
    )
```

```python
import functools

import jax
import jax.numpy as jnp
from jax import lax
from jax.experimental import pallas as pl
from jax.experimental.pallas import tpu as pltpu
from jax.sharding import Mesh
from jax.sharding import PartitionSpec as P

F32 = jnp.float32
BF16 = jnp.bfloat16
SEQ = ("y", "z", "c")
VMEM_LIMIT = 32 * 1024 * 1024


def swap_core(value):
    return lax.ppermute(value, "c", [(0, 1), (1, 0)])


def swap_x(value, k):
    return lax.ppermute(value, "x", [(i, i ^ k) for i in range(4)])


def swap_near(value, first):
    steps = (1, 3) if first else (3, 1)
    return lax.ppermute(
        value, ("c", "x"), [(c * 4 + x, c * 4 + (x ^ steps[c])) for c in range(2) for x in range(4)]
    )


def swap_first(value, k, first=True):
    pairs = []
    for index in range(32):
        along_z = (index % 2 == 0) == first
        pairs.append((index, index ^ (2 * k if along_z else 8 * k)))
    return lax.ppermute(value, SEQ, pairs)


def swap_second(value, k):
    return swap_first(value, k, False)


def dot(a, b):
    return jnp.dot(a, b, preferred_element_type=F32)


def dot_t(a, b):
    return lax.dot_general(a, b, (((1,), (1,)), ((), ())), preferred_element_type=F32)


def call(body, outs, inputs, scalars=(), flops=0, scratch=(), outside=False):
    specs = [pl.BlockSpec(memory_space=pltpu.SMEM)] * len(scalars)
    specs += [pl.BlockSpec(memory_space=pltpu.HBM if outside else pltpu.VMEM)] * len(inputs)
    moved = sum(v.size * v.dtype.itemsize for v in list(inputs) + list(outs))
    return pl.pallas_call(
        body,
        out_shape=outs,
        in_specs=specs,
        out_specs=[pl.BlockSpec(memory_space=pltpu.VMEM)] * len(outs),
        scratch_shapes=list(scratch),
        compiler_params=pltpu.CompilerParams(vmem_limit_bytes=60 * 1024 * 1024 if outside else VMEM_LIMIT),
        cost_estimate=pl.CostEstimate(flops=flops, bytes_accessed=moved, transcendentals=0),
    )(*scalars, *inputs)


def shape(dims, dtype):
    return jax.ShapeDtypeStruct(dims, dtype)


def bounds(lengths):
    count = lengths.shape[1]
    row = lax.broadcasted_iota(jnp.int32, (count, count), 0)
    column = lax.broadcasted_iota(jnp.int32, (count, count), 1)
    wide = jnp.broadcast_to(lengths, (count, count)).astype(F32)
    ends = jnp.sum(jnp.where(column <= row, wide, 0.0), axis=1, keepdims=True)
    size = jnp.sum(jnp.where(column == row, wide, 0.0), axis=1, keepdims=True)
    return ends - size, ends, size


def membership(lengths, length):
    starts, ends, size = bounds(lengths)
    count = lengths.shape[1]
    position = lax.broadcasted_iota(jnp.int32, (count, length), 1).astype(F32)
    inside = (position >= starts) & (position < ends)
    return jnp.where(inside, 1.0, 0.0).astype(BF16), size


def pool_kernel(lengths, states, cots, pooled):
    pooling, size = membership(lengths[...], states.shape[0])
    width = states.shape[1]
    pooled[:, :width] = (dot(pooling, states[...]) / size).astype(BF16)
    pooled[:, width:] = dot(pooling, cots[...]).astype(BF16)


def stack_kernel(own, one, two, three, out):
    span = own.shape[0]
    for k, block in enumerate((own, one, two, three)):
        out[k * span : (k + 1) * span] = block[...]


def cut_products(count, offsets, whole, keep, send):
    part = keep.shape[0] // (2 * count)
    for k in range(4):
        out = keep if k < 2 else send
        for i in range(count):
            place = pl.multiple_of(offsets[k] + i * 4 * part, 16)
            to = (k % 2) * count * part + i * part
            out[to : to + part] = whole[pl.ds(place, part), :]


def product_kernel(offsets, *refs):
    sources, (keep, send), (w_enc, w_gate, w_lift, w_down, w_dec, whole, sems) = (
        refs[:5],
        refs[5:7],
        refs[7:],
    )
    targets = (w_enc, w_gate, w_lift, w_down, w_dec)
    copies = [
        pltpu.make_async_copy(source, target, sems.at[i])
        for i, (source, target) in enumerate(zip(sources, targets))
    ]
    for copy in copies:
        copy.start()
    hid = w_gate.shape[0]
    copies[0].wait()
    copies[1].wait()
    whole[:hid] = dot_t(w_gate[...], w_enc[...]).astype(BF16)
    copies[2].wait()
    whole[hid : 2 * hid] = dot_t(w_lift[...], w_enc[...]).astype(BF16)
    copies[3].wait()
    copies[4].wait()
    whole[2 * hid :] = dot(w_down[...], w_dec[...]).astype(BF16)
    cut_products(3, offsets, whole, keep, send)


def encode_kernel(w_dec, w_enc, pooled, rep, back):
    width = w_enc.shape[0]
    rep[...] = dot(pooled[:, :width], w_enc[...]).astype(BF16)
    back[...] = dot_t(dot_t(pooled[:, width:], w_dec[...]).astype(BF16), w_enc[...])


def halve_kernel(keep, first, own, send):
    half = own.shape[0]
    own[...] = keep[:half].astype(F32) + first[:half].astype(F32)
    send[...] = (keep[half:].astype(F32) + first[half:].astype(F32)).astype(BF16)


def hidden_rows(rows, products):
    width = products.shape[1]
    part = products.shape[0] // 3
    stacked = [block[...] for block in rows]
    stacked = jnp.concatenate(stacked, axis=0)
    both = dot_t(products[: 2 * part], stacked[:, :width])
    grad_hidden = dot_t(products[2 * part :], stacked[:, width:])
    gate, lift = both[:part], both[part:]
    sig = 1.0 / (1.0 + jnp.exp(-gate))
    silu = gate * sig
    grad_gate = grad_hidden * lift * sig * (1.0 + gate * (1.0 - sig))
    grads = jnp.concatenate([grad_gate, grad_hidden * silu], axis=0).astype(BF16)
    return (silu * lift).astype(BF16), dot(grads.T, products[: 2 * part])


def near_kernel(r0, r1, r2, r3, own, second, products, hidden, partial):
    products[...] = (own[...] + second[...].astype(F32)).astype(BF16)
    hidden[...], partial[...] = hidden_rows((r0, r1, r2, r3), products)


def far_kernel(r0, r1, r2, r3, products, near_hidden, hidden, partial):
    half = near_hidden.shape[1]
    hidden[:, :half] = near_hidden[...]
    hidden[:, half:], terms = hidden_rows((r0, r1, r2, r3), products)
    partial[...] = terms.astype(BF16)


def place_blocks(total, outs):
    patches = total.shape[0] // 16
    for first, out in enumerate(outs):
        for second in range(4):
            place = (4 * second + first) * patches
            out[second * patches : (second + 1) * patches] = total[place : place + patches].astype(BF16)


def pair_kernel(own, second, out):
    part = own.shape[0]
    out[:part] = own[...]
    out[part:] = second[...]


def stack_hidden(offsets, own, second, others, low, stack):
    part, span = own.shape[0], stack.shape[1]
    blocks = (own, second, others.at[:part], others.at[part:])
    for k, block in enumerate(blocks):
        place = pl.multiple_of(offsets[k], 16)
        stack[pl.ds(place, part), :] = block[:, low : low + span]


def down_far_kernel(offsets, own, second, others, w_down, out, stack):
    stack_hidden(offsets, own, second, others, out.shape[0], stack)
    out[...] = dot(stack[...].T, w_down[...]).astype(BF16)


def grad_near_kernel(partial, other, *outs):
    place_blocks(partial[...] + other[...].astype(F32), outs)


def down_near_kernel(offsets, own, second, others, w_down, other, *rest):
    stack = rest[-1]
    stack_hidden(offsets, own, second, others, 0, stack)
    place_blocks(dot(stack[...].T, w_down[...]) + other[...].astype(F32), rest[:-1])


def add_kernel(*refs):
    terms, outs = refs[:8], refs[8:]
    patches, width = terms[0].shape[0] // 4, terms[0].shape[1]
    for i in range(2):
        total = sum(term[...].astype(F32) for term in terms[4 * i : 4 * i + 4])
        for k, out in enumerate(outs):
            rows = total[k * patches : (k + 1) * patches]
            out[:, i * width : (i + 1) * width] = rows.astype(out.dtype)


def decode_kernel(own, one, two, three, rep, back, weight, owners, partial, outgoing):
    width = rep.shape[1]
    total = own[...] + one[...].astype(F32) + two[...].astype(F32) + three[...].astype(F32)
    states = (total[:, :width] + rep[...].astype(F32)).astype(BF16)
    partial[:, : weight.shape[1]] = dot(states, weight[...]).astype(BF16)
    partial[:, weight.shape[1] :] = (total[:, width:] + back[...]).astype(BF16)
    count = rep.shape[0]
    own_row = jnp.broadcast_to(owners[...], (count, count))
    row = lax.broadcasted_iota(jnp.int32, (count, count), 0)
    column = lax.broadcasted_iota(jnp.int32, (count, count), 1)
    own_column = jnp.sum(jnp.where(row == column, own_row, 0), axis=1, keepdims=True)
    same = jnp.where((own_column == own_row) & (row < column), 1, 0)
    rank = jnp.sum(same, axis=0, keepdims=True)
    targets = 2 * owners[...] + rank
    slots = lax.broadcasted_iota(jnp.int32, (2 * count, count), 0)
    routing = jnp.where(slots == targets, 1.0, 0.0).astype(BF16)
    outgoing[...] = dot(routing, states).astype(BF16)


def finish_kernel(lengths, states, cots, own, one, two, three, out, grad):
    total = (
        own[...].astype(F32) + one[...].astype(F32) + two[...].astype(F32) + three[...].astype(F32)
    )
    pooling, size = membership(lengths[...], states.shape[0])
    width = states.shape[1]
    pick = (((0,), (0,)), ((), ()))
    twice = jnp.concatenate([pooling, pooling], axis=0)
    for values, result, part in (
        (states, out, total[:, :width]),
        (cots, grad, total[:, width:] / size),
    ):
        high = part.astype(BF16)
        low = (part - high.astype(F32)).astype(BF16)
        both = jnp.concatenate([high, low], axis=0)
        spread = lax.dot_general(twice, both, pick, preferred_element_type=F32)
        result[...] = (values[...].astype(F32) + spread).astype(BF16)


def on_device(
    byte_states, patch_lengths, patch_owner, w_enc, w_gate, w_lift, w_down, w_dec, byte_cot
):
    patches = patch_lengths.shape[1]
    width = byte_states.shape[1]
    latent = w_enc.shape[1]
    hid = w_gate.shape[1]
    part = hid // 4
    group = 16 * patches
    x, core = lax.axis_index("x"), lax.axis_index("c")
    step = jnp.where(core == 0, 1, 3)
    halving = (jnp.stack([x, x ^ step ^ 2, x ^ step, x ^ 2]) * part).astype(jnp.int32)
    owners = patch_owner.reshape(1, patches)
    w_gate, w_lift = w_gate.T, w_lift.T

    def after(value, token):
        return lax.optimization_barrier((value, token))[0]

    def over(swap, own, *sends):
        sends = sends or (own,) * 3
        two, one, three = [swap(sends[k - 1], k) for k in (2, 1, 3)]
        return [own, one, two, three]

    def halve(keep, first):
        own, send = call(
            halve_kernel,
            [shape((keep.shape[0] // 2, width), F32), shape((keep.shape[0] // 2, width), BF16)],
            [keep, first],
            flops=2 * keep.size,
        )
        return own, swap_near(send, False)

    weights = [w_enc, w_gate, w_lift, w_down, w_dec]
    keep, send = call(
        product_kernel,
        [shape((6 * part, width), BF16)] * 2,
        weights,
        [halving],
        flops=6 * hid * width * latent,
        scratch=[pltpu.VMEM(w.shape, BF16) for w in weights]
        + [pltpu.VMEM((3 * hid, width), BF16), pltpu.SemaphoreType.DMA((5,))],
        outside=True,
    )
    first = swap_near(send, True)
    (pooled,) = call(
        pool_kernel,
        [shape((patches, 2 * width), BF16)],
        [patch_lengths, after(byte_states, send), byte_cot],
        flops=4 * patches * byte_states.size,
    )
    (rows,) = call(
        stack_kernel,
        [shape((4 * patches, 2 * width), BF16)],
        over(swap_first, pooled),
        flops=8 * patches * width,
    )
    near = over(swap_second, rows)
    far = [swap_core(block) for block in near]
    own, second = halve(keep, first)
    flops = 4 * group * width * part
    products, near_hidden, near_partial = call(
        near_kernel,
        [
            shape((3 * part, width), BF16),
            shape((part, group), BF16),
            shape((group, width), F32),
        ],
        [*near, own, second],
        flops=3 * flops,
    )
    hidden, far_partial = call(
        far_kernel,
        [shape((part, 2 * group), BF16), shape((group, width), BF16)],
        [*far, products, near_hidden],
        flops=3 * flops,
    )
    hidden_second = swap_near(hidden, False)
    (pair,) = call(pair_kernel, [shape((2 * part, 2 * group), BF16)], [hidden, hidden_second])
    hiddens = [hidden, hidden_second, swap_near(pair, True)]
    grad_terms = call(
        grad_near_kernel,
        [shape((4 * patches, width), BF16)] * 4,
        [near_partial, swap_core(far_partial)],
        flops=near_partial.size,
    )
    grad_first = over(swap_first, *grad_terms)
    patch_rep, back = call(
        encode_kernel,
        [shape((patches, latent), BF16), shape((patches, width), F32)],
        [w_dec, w_enc, pooled],
        flops=6 * patches * width * latent,
    )
    (far_rows,) = call(
        down_far_kernel,
        [shape((group, latent), BF16)],
        [*hiddens, after(w_down, (*grad_terms, back))],
        [halving],
        flops=2 * group * latent * hid,
        scratch=[pltpu.VMEM((hid, group), BF16)],
    )
    terms = call(
        down_near_kernel,
        [shape((4 * patches, latent), BF16)] * 4,
        [*hiddens, w_down, swap_core(far_rows)],
        [halving],
        flops=2 * group * latent * hid,
        scratch=[pltpu.VMEM((hid, group), BF16)],
    )
    own, *sends = call(
        add_kernel,
        [shape((patches, latent + width), F32)] + [shape((patches, latent + width), BF16)] * 3,
        over(swap_first, *terms) + grad_first,
        flops=32 * patches * width,
    )
    partial, outgoing = call(
        decode_kernel,
        [shape((patches, 2 * width), BF16), shape((2 * patches, latent), BF16)],
        [*over(swap_second, own, *sends), patch_rep, back, w_dec, owners],
        flops=2 * patches * width * latent,
    )
    latent_states = lax.all_to_all(outgoing, SEQ, split_axis=0, concat_axis=0, tiled=True)
    partials = over(swap_x, partial)
    byte_out, byte_grad = call(
        finish_kernel,
        [shape(byte_states.shape, BF16), shape(byte_cot.shape, BF16)],
        [patch_lengths, byte_states, byte_cot, *partials],
        flops=16 * patches * byte_states.size,
    )
    return byte_out, byte_grad, latent_states


def solution(mesh):
    fine = Mesh(mesh.devices.reshape(4, 4, 2, 4), ("y", "z", "c", "x"))
    return jax.shard_map(
        on_device,
        mesh=fine,
        in_specs=(
            P(SEQ, None),
            P(SEQ, None),
            P(SEQ, None),
            P(None, "x"),
            P("x", SEQ),
            P("x", SEQ),
            P(SEQ, "x"),
            P("x", None),
            P(SEQ, None),
        ),
        out_specs=(P(SEQ, None), P(SEQ, None), P(SEQ, "x")),
        check_vma=False,
    )
```

```python
import functools

import jax
import jax.numpy as jnp
from jax import lax
from jax.experimental import pallas as pl
from jax.experimental.pallas import tpu as pltpu
from jax.sharding import Mesh
from jax.sharding import PartitionSpec as P

F32 = jnp.float32
BF16 = jnp.bfloat16
SEQ = ("y", "z", "c")
VMEM_LIMIT = 32 * 1024 * 1024


def swap_core(value):
    return lax.ppermute(value, "c", [(0, 1), (1, 0)])


def swap_x(value, k):
    return lax.ppermute(value, "x", [(i, i ^ k) for i in range(4)])


def swap_near(value, first):
    steps = (1, 3) if first else (3, 1)
    return lax.ppermute(
        value, ("c", "x"), [(c * 4 + x, c * 4 + (x ^ steps[c])) for c in range(2) for x in range(4)]
    )


def swap_first(value, k, first=True):
    pairs = []
    for index in range(32):
        along_z = (index % 2 == 0) == first
        pairs.append((index, index ^ (2 * k if along_z else 8 * k)))
    return lax.ppermute(value, SEQ, pairs)


def swap_second(value, k):
    return swap_first(value, k, False)


def dot(a, b):
    return jnp.dot(a, b, preferred_element_type=F32)


def dot_t(a, b):
    return lax.dot_general(a, b, (((1,), (1,)), ((), ())), preferred_element_type=F32)


def call(body, outs, inputs, scalars=(), flops=0, scratch=(), outside=False):
    specs = [pl.BlockSpec(memory_space=pltpu.SMEM)] * len(scalars)
    specs += [pl.BlockSpec(memory_space=pltpu.HBM if outside else pltpu.VMEM)] * len(inputs)
    moved = sum(v.size * v.dtype.itemsize for v in list(inputs) + list(outs))
    return pl.pallas_call(
        body,
        out_shape=outs,
        in_specs=specs,
        out_specs=[pl.BlockSpec(memory_space=pltpu.VMEM)] * len(outs),
        scratch_shapes=list(scratch),
        compiler_params=pltpu.CompilerParams(vmem_limit_bytes=60 * 1024 * 1024 if outside else VMEM_LIMIT),
        cost_estimate=pl.CostEstimate(flops=flops, bytes_accessed=moved, transcendentals=0),
    )(*scalars, *inputs)


def shape(dims, dtype):
    return jax.ShapeDtypeStruct(dims, dtype)


def bounds(lengths):
    count = lengths.shape[1]
    row = lax.broadcasted_iota(jnp.int32, (count, count), 0)
    column = lax.broadcasted_iota(jnp.int32, (count, count), 1)
    wide = jnp.broadcast_to(lengths, (count, count)).astype(F32)
    ends = jnp.sum(jnp.where(column <= row, wide, 0.0), axis=1, keepdims=True)
    size = jnp.sum(jnp.where(column == row, wide, 0.0), axis=1, keepdims=True)
    return ends - size, ends, size


def membership(lengths, length):
    starts, ends, size = bounds(lengths)
    count = lengths.shape[1]
    position = lax.broadcasted_iota(jnp.int32, (count, length), 1).astype(F32)
    inside = (position >= starts) & (position < ends)
    return jnp.where(inside, 1.0, 0.0).astype(BF16), size


def pool_kernel(lengths, states, cots, pooled):
    pooling, size = membership(lengths[...], states.shape[0])
    width = states.shape[1]
    pooled[:, :width] = (dot(pooling, states[...]) / size).astype(BF16)
    pooled[:, width:] = dot(pooling, cots[...]).astype(BF16)


def stack_kernel(own, one, two, three, out):
    span = own.shape[0]
    for k, block in enumerate((own, one, two, three)):
        out[k * span : (k + 1) * span] = block[...]


def cut_products(count, offsets, whole, keep, send):
    part = keep.shape[0] // (2 * count)
    for k in range(4):
        out = keep if k < 2 else send
        for i in range(count):
            place = pl.multiple_of(offsets[k] + i * 4 * part, 16)
            to = (k % 2) * count * part + i * part
            out[to : to + part] = whole[pl.ds(place, part), :]


def product_kernel(offsets, *refs):
    sources, (keep, send), (w_enc, w_gate, w_lift, w_down, w_dec, whole, sems) = (
        refs[:5],
        refs[5:7],
        refs[7:],
    )
    targets = (w_enc, w_gate, w_lift, w_down, w_dec)
    copies = [
        pltpu.make_async_copy(source, target, sems.at[i])
        for i, (source, target) in enumerate(zip(sources, targets))
    ]
    for copy in copies:
        copy.start()
    hid = w_gate.shape[0]
    copies[0].wait()
    copies[1].wait()
    whole[:hid] = dot_t(w_gate[...], w_enc[...]).astype(BF16)
    copies[2].wait()
    whole[hid : 2 * hid] = dot_t(w_lift[...], w_enc[...]).astype(BF16)
    copies[3].wait()
    copies[4].wait()
    whole[2 * hid :] = dot(w_down[...], w_dec[...]).astype(BF16)
    cut_products(3, offsets, whole, keep, send)


def encode_kernel(w_dec, w_enc, pooled, rep, back):
    width = w_enc.shape[0]
    rep[...] = dot(pooled[:, :width], w_enc[...]).astype(BF16)
    back[...] = dot_t(dot_t(pooled[:, width:], w_dec[...]).astype(BF16), w_enc[...])


def halve_kernel(keep, first, own, send):
    half = own.shape[0]
    own[...] = keep[:half].astype(F32) + first[:half].astype(F32)
    send[...] = (keep[half:].astype(F32) + first[half:].astype(F32)).astype(BF16)


def hidden_rows(rows, products):
    width = products.shape[1]
    part = products.shape[0] // 3
    stacked = [block[...] for block in rows]
    stacked = jnp.concatenate(stacked, axis=0)
    both = dot_t(products[: 2 * part], stacked[:, :width])
    grad_hidden = dot_t(products[2 * part :], stacked[:, width:])
    gate, lift = both[:part], both[part:]
    sig = 1.0 / (1.0 + jnp.exp(-gate))
    silu = gate * sig
    grad_gate = grad_hidden * lift * sig * (1.0 + gate * (1.0 - sig))
    grads = jnp.concatenate([grad_gate, grad_hidden * silu], axis=0).astype(BF16)
    return (silu * lift).astype(BF16), dot(grads.T, products[: 2 * part])


def near_kernel(r0, r1, r2, r3, own, second, products, hidden, partial):
    products[...] = (own[...] + second[...].astype(F32)).astype(BF16)
    hidden[...], partial[...] = hidden_rows((r0, r1, r2, r3), products)


def far_kernel(r0, r1, r2, r3, products, near_hidden, hidden, partial):
    half = near_hidden.shape[1]
    hidden[:, :half] = near_hidden[...]
    hidden[:, half:], terms = hidden_rows((r0, r1, r2, r3), products)
    partial[...] = terms.astype(BF16)


def place_blocks(total, outs):
    patches = total.shape[0] // 16
    for first, out in enumerate(outs):
        for second in range(4):
            place = (4 * second + first) * patches
            out[second * patches : (second + 1) * patches] = total[place : place + patches].astype(BF16)


def pair_kernel(own, second, out):
    part = own.shape[0]
    out[:part] = own[...]
    out[part:] = second[...]


def stack_hidden(offsets, own, second, others, low, stack):
    part, span = own.shape[0], stack.shape[1]
    blocks = (own, second, others.at[:part], others.at[part:])
    for k, block in enumerate(blocks):
        place = pl.multiple_of(offsets[k], 16)
        stack[pl.ds(place, part), :] = block[:, low : low + span]


def down_far_kernel(offsets, own, second, others, w_down, out, stack):
    stack_hidden(offsets, own, second, others, out.shape[0], stack)
    out[...] = dot(stack[...].T, w_down[...]).astype(BF16)


def grad_near_kernel(partial, other, *outs):
    place_blocks(partial[...] + other[...].astype(F32), outs)


def down_near_kernel(offsets, own, second, others, w_down, other, *rest):
    stack = rest[-1]
    stack_hidden(offsets, own, second, others, 0, stack)
    place_blocks(dot(stack[...].T, w_down[...]) + other[...].astype(F32), rest[:-1])


def add_kernel(*refs):
    terms, outs = refs[:8], refs[8:]
    patches, width = terms[0].shape[0] // 4, terms[0].shape[1]
    for i in range(2):
        total = sum(term[...].astype(F32) for term in terms[4 * i : 4 * i + 4])
        for k, out in enumerate(outs):
            rows = total[k * patches : (k + 1) * patches]
            out[:, i * width : (i + 1) * width] = rows.astype(out.dtype)


def decode_kernel(own, one, two, three, rep, back, weight, owners, partial, outgoing):
    width = rep.shape[1]
    total = own[...] + one[...].astype(F32) + two[...].astype(F32) + three[...].astype(F32)
    states = (total[:, :width] + rep[...].astype(F32)).astype(BF16)
    partial[:, : weight.shape[1]] = dot(states, weight[...]).astype(BF16)
    partial[:, weight.shape[1] :] = (total[:, width:] + back[...]).astype(BF16)
    count = rep.shape[0]
    own_row = jnp.broadcast_to(owners[...], (count, count))
    row = lax.broadcasted_iota(jnp.int32, (count, count), 0)
    column = lax.broadcasted_iota(jnp.int32, (count, count), 1)
    own_column = jnp.sum(jnp.where(row == column, own_row, 0), axis=1, keepdims=True)
    same = jnp.where((own_column == own_row) & (row < column), 1, 0)
    rank = jnp.sum(same, axis=0, keepdims=True)
    targets = 2 * owners[...] + rank
    slots = lax.broadcasted_iota(jnp.int32, (2 * count, count), 0)
    routing = jnp.where(slots == targets, 1.0, 0.0).astype(BF16)
    outgoing[...] = dot(routing, states).astype(BF16)


def finish_kernel(lengths, states, cots, own, one, two, three, out, grad):
    total = (
        own[...].astype(F32) + one[...].astype(F32) + two[...].astype(F32) + three[...].astype(F32)
    )
    pooling, size = membership(lengths[...], states.shape[0])
    width = states.shape[1]
    pick = (((0,), (0,)), ((), ()))
    twice = jnp.concatenate([pooling, pooling], axis=0)
    for values, result, part in (
        (states, out, total[:, :width]),
        (cots, grad, total[:, width:] / size),
    ):
        high = part.astype(BF16)
        low = (part - high.astype(F32)).astype(BF16)
        both = jnp.concatenate([high, low], axis=0)
        spread = lax.dot_general(twice, both, pick, preferred_element_type=F32)
        result[...] = (values[...].astype(F32) + spread).astype(BF16)


def on_device(
    byte_states, patch_lengths, patch_owner, w_enc, w_gate, w_lift, w_down, w_dec, byte_cot
):
    patches = patch_lengths.shape[1]
    width = byte_states.shape[1]
    latent = w_enc.shape[1]
    hid = w_gate.shape[1]
    part = hid // 4
    group = 16 * patches
    x, core = lax.axis_index("x"), lax.axis_index("c")
    step = jnp.where(core == 0, 1, 3)
    halving = (jnp.stack([x, x ^ step ^ 2, x ^ step, x ^ 2]) * part).astype(jnp.int32)
    owners = patch_owner.reshape(1, patches)
    w_gate, w_lift = w_gate.T, w_lift.T

    def after(value, token):
        return lax.optimization_barrier((value, token))[0]

    def over(swap, own, *sends):
        sends = sends or (own,) * 3
        two, one, three = [swap(sends[k - 1], k) for k in (2, 1, 3)]
        return [own, one, two, three]

    def halve(keep, first):
        own, send = call(
            halve_kernel,
            [shape((keep.shape[0] // 2, width), F32), shape((keep.shape[0] // 2, width), BF16)],
            [keep, first],
            flops=2 * keep.size,
        )
        return own, swap_near(send, False)

    weights = [w_enc, w_gate, w_lift, w_down, w_dec]
    keep, send = call(
        product_kernel,
        [shape((6 * part, width), BF16)] * 2,
        weights,
        [halving],
        flops=6 * hid * width * latent,
        scratch=[pltpu.VMEM(w.shape, BF16) for w in weights]
        + [pltpu.VMEM((3 * hid, width), BF16), pltpu.SemaphoreType.DMA((5,))],
        outside=True,
    )
    first = swap_near(send, True)
    (pooled,) = call(
        pool_kernel,
        [shape((patches, 2 * width), BF16)],
        [patch_lengths, after(byte_states, send), byte_cot],
        flops=4 * patches * byte_states.size,
    )
    (rows,) = call(
        stack_kernel,
        [shape((4 * patches, 2 * width), BF16)],
        over(swap_first, pooled),
        flops=8 * patches * width,
    )
    near = over(swap_second, rows)
    far = [swap_core(block) for block in near]
    own, second = halve(keep, first)
    flops = 4 * group * width * part
    products, near_hidden, near_partial = call(
        near_kernel,
        [
            shape((3 * part, width), BF16),
            shape((part, group), BF16),
            shape((group, width), F32),
        ],
        [*near, own, second],
        flops=3 * flops,
    )
    hidden, far_partial = call(
        far_kernel,
        [shape((part, 2 * group), BF16), shape((group, width), BF16)],
        [*far, products, near_hidden],
        flops=3 * flops,
    )
    hidden_second = swap_near(hidden, False)
    (pair,) = call(pair_kernel, [shape((2 * part, 2 * group), BF16)], [hidden, hidden_second])
    hiddens = [hidden, hidden_second, swap_near(pair, True)]
    grad_terms = call(
        grad_near_kernel,
        [shape((4 * patches, width), BF16)] * 4,
        [near_partial, swap_core(far_partial)],
        flops=near_partial.size,
    )
    grad_first = over(swap_first, *grad_terms)
    patch_rep, back = call(
        encode_kernel,
        [shape((patches, latent), BF16), shape((patches, width), F32)],
        [w_dec, w_enc, pooled],
        flops=6 * patches * width * latent,
    )
    (far_rows,) = call(
        down_far_kernel,
        [shape((group, latent), BF16)],
        [*hiddens, after(w_down, (grad_first[1], back))],
        [halving],
        flops=2 * group * latent * hid,
        scratch=[pltpu.VMEM((hid, group), BF16)],
    )
    terms = call(
        down_near_kernel,
        [shape((4 * patches, latent), BF16)] * 4,
        [*hiddens, w_down, swap_core(far_rows)],
        [halving],
        flops=2 * group * latent * hid,
        scratch=[pltpu.VMEM((hid, group), BF16)],
    )
    own, *sends = call(
        add_kernel,
        [shape((patches, latent + width), F32)] + [shape((patches, latent + width), BF16)] * 3,
        over(swap_first, *terms) + grad_first,
        flops=32 * patches * width,
    )
    partial, outgoing = call(
        decode_kernel,
        [shape((patches, 2 * width), BF16), shape((2 * patches, latent), BF16)],
        [*over(swap_second, own, *sends), patch_rep, back, w_dec, owners],
        flops=2 * patches * width * latent,
    )
    latent_states = lax.all_to_all(outgoing, SEQ, split_axis=0, concat_axis=0, tiled=True)
    partials = over(swap_x, partial)
    byte_out, byte_grad = call(
        finish_kernel,
        [shape(byte_states.shape, BF16), shape(byte_cot.shape, BF16)],
        [patch_lengths, byte_states, byte_cot, *partials],
        flops=16 * patches * byte_states.size,
    )
    return byte_out, byte_grad, latent_states


def solution(mesh):
    fine = Mesh(mesh.devices.reshape(4, 4, 2, 4), ("y", "z", "c", "x"))
    return jax.shard_map(
        on_device,
        mesh=fine,
        in_specs=(
            P(SEQ, None),
            P(SEQ, None),
            P(SEQ, None),
            P(None, "x"),
            P("x", SEQ),
            P("x", SEQ),
            P(SEQ, "x"),
            P("x", None),
            P(SEQ, None),
        ),
        out_specs=(P(SEQ, None), P(SEQ, None), P(SEQ, "x")),
        check_vma=False,
    )
```

```python
import functools

import jax
import jax.numpy as jnp
from jax import lax
from jax.experimental import pallas as pl
from jax.experimental.pallas import tpu as pltpu
from jax.sharding import Mesh
from jax.sharding import PartitionSpec as P

F32 = jnp.float32
BF16 = jnp.bfloat16
SEQ = ("y", "z", "c")
VMEM_LIMIT = 32 * 1024 * 1024


def swap_core(value):
    return lax.ppermute(value, "c", [(0, 1), (1, 0)])


def swap_x(value, k):
    return lax.ppermute(value, "x", [(i, i ^ k) for i in range(4)])


def swap_near(value, first):
    steps = (1, 3) if first else (3, 1)
    return lax.ppermute(
        value, ("c", "x"), [(c * 4 + x, c * 4 + (x ^ steps[c])) for c in range(2) for x in range(4)]
    )


def swap_first(value, k, first=True):
    pairs = []
    for index in range(32):
        along_z = (index % 2 == 0) == first
        pairs.append((index, index ^ (2 * k if along_z else 8 * k)))
    return lax.ppermute(value, SEQ, pairs)


def swap_second(value, k):
    return swap_first(value, k, False)


def dot(a, b):
    return jnp.dot(a, b, preferred_element_type=F32)


def dot_t(a, b):
    return lax.dot_general(a, b, (((1,), (1,)), ((), ())), preferred_element_type=F32)


def call(body, outs, inputs, scalars=(), flops=0, scratch=(), outside=False):
    specs = [pl.BlockSpec(memory_space=pltpu.SMEM)] * len(scalars)
    specs += [pl.BlockSpec(memory_space=pltpu.HBM if outside else pltpu.VMEM)] * len(inputs)
    moved = sum(v.size * v.dtype.itemsize for v in list(inputs) + list(outs))
    return pl.pallas_call(
        body,
        out_shape=outs,
        in_specs=specs,
        out_specs=[pl.BlockSpec(memory_space=pltpu.VMEM)] * len(outs),
        scratch_shapes=list(scratch),
        compiler_params=pltpu.CompilerParams(vmem_limit_bytes=60 * 1024 * 1024 if outside else VMEM_LIMIT),
        cost_estimate=pl.CostEstimate(flops=flops, bytes_accessed=moved, transcendentals=0),
    )(*scalars, *inputs)


def shape(dims, dtype):
    return jax.ShapeDtypeStruct(dims, dtype)


def bounds(lengths):
    count = lengths.shape[1]
    row = lax.broadcasted_iota(jnp.int32, (count, count), 0)
    column = lax.broadcasted_iota(jnp.int32, (count, count), 1)
    wide = jnp.broadcast_to(lengths, (count, count)).astype(F32)
    ends = jnp.sum(jnp.where(column <= row, wide, 0.0), axis=1, keepdims=True)
    size = jnp.sum(jnp.where(column == row, wide, 0.0), axis=1, keepdims=True)
    return ends - size, ends, size


def membership(lengths, length):
    starts, ends, size = bounds(lengths)
    count = lengths.shape[1]
    position = lax.broadcasted_iota(jnp.int32, (count, length), 1).astype(F32)
    inside = (position >= starts) & (position < ends)
    return jnp.where(inside, 1.0, 0.0).astype(BF16), size


def pool_kernel(lengths, states, cots, pooled):
    pooling, size = membership(lengths[...], states.shape[0])
    width = states.shape[1]
    pooled[:, :width] = (dot(pooling, states[...]) / size).astype(BF16)
    pooled[:, width:] = dot(pooling, cots[...]).astype(BF16)


def stack_kernel(own, one, two, three, out):
    span = own.shape[0]
    for k, block in enumerate((own, one, two, three)):
        out[k * span : (k + 1) * span] = block[...]


def block_offsets(part):
    x = lax.axis_index("x")
    step = jnp.where(lax.axis_index("c") == 0, 1, 3)
    return [x * part, (x ^ step ^ 2) * part, (x ^ step) * part, (x ^ 2) * part]


def cut_products(count, whole, keep, send):
    part = keep.shape[0] // (2 * count)
    offsets = block_offsets(part)
    for k in range(4):
        out = keep if k < 2 else send
        for i in range(count):
            place = pl.multiple_of(offsets[k] + i * 4 * part, 16)
            to = (k % 2) * count * part + i * part
            out[to : to + part] = whole[pl.ds(place, part), :]


def product_kernel(*refs):
    sources, (keep, send), (w_enc, w_gate, w_lift, w_down, w_dec, whole, sems) = (
        refs[:5],
        refs[5:7],
        refs[7:],
    )
    targets = (w_enc, w_gate, w_lift, w_down, w_dec)
    half = w_enc.shape[0] // 2
    pairs = list(zip(sources[1:], targets[1:]))
    pairs[1:1] = [
        (sources[0].at[pl.ds(i * half, half)], w_enc.at[pl.ds(i * half, half)]) for i in range(2)
    ]
    copies = [
        pltpu.make_async_copy(source, target, sems.at[i])
        for i, (source, target) in enumerate(pairs)
    ]
    for copy in copies:
        copy.start()
    hid = w_gate.shape[0]
    copies[0].wait()
    for i in range(2):
        copies[1 + i].wait()
        columns = slice(i * half, (i + 1) * half)
        whole[:hid, columns] = dot_t(w_gate[...], w_enc[columns]).astype(BF16)
    copies[3].wait()
    whole[hid : 2 * hid] = dot_t(w_lift[...], w_enc[...]).astype(BF16)
    copies[4].wait()
    copies[5].wait()
    whole[2 * hid :] = dot(w_down[...], w_dec[...]).astype(BF16)
    cut_products(3, whole, keep, send)


def encode_kernel(w_dec, w_enc, pooled, rep, back):
    width = w_enc.shape[0]
    rep[...] = dot(pooled[:, :width], w_enc[...]).astype(BF16)
    back[...] = dot_t(dot_t(pooled[:, width:], w_dec[...]).astype(BF16), w_enc[...])


def halve_kernel(keep, first, own, send):
    half = own.shape[0]
    own[...] = keep[:half].astype(F32) + first[:half].astype(F32)
    send[...] = (keep[half:].astype(F32) + first[half:].astype(F32)).astype(BF16)


def hidden_rows(rows, products):
    width = products.shape[1]
    part = products.shape[0] // 3
    stacked = [block[...] for block in rows]
    stacked = jnp.concatenate(stacked, axis=0)
    both = dot_t(products[: 2 * part], stacked[:, :width])
    grad_hidden = dot_t(products[2 * part :], stacked[:, width:])
    gate, lift = both[:part], both[part:]
    sig = 1.0 / (1.0 + jnp.exp(-gate))
    silu = gate * sig
    grad_gate = grad_hidden * lift * sig * (1.0 + gate * (1.0 - sig))
    grads = jnp.concatenate([grad_gate, grad_hidden * silu], axis=0).astype(BF16)
    return (silu * lift).astype(BF16), dot(grads.T, products[: 2 * part])


def near_kernel(r0, r1, r2, r3, own, second, products, hidden, partial):
    products[...] = (own[...] + second[...].astype(F32)).astype(BF16)
    hidden[...], partial[...] = hidden_rows((r0, r1, r2, r3), products)


def far_kernel(r0, r1, r2, r3, products, near_hidden, hidden, partial):
    half = near_hidden.shape[1]
    hidden[:, :half] = near_hidden[...]
    hidden[:, half:], terms = hidden_rows((r0, r1, r2, r3), products)
    partial[...] = terms.astype(BF16)


def place_blocks(total, outs):
    patches = total.shape[0] // 16
    for first, out in enumerate(outs):
        for second in range(4):
            place = (4 * second + first) * patches
            out[second * patches : (second + 1) * patches] = total[place : place + patches].astype(BF16)


def pair_kernel(own, second, out):
    part = own.shape[0]
    out[:part] = own[...]
    out[part:] = second[...]


def stack_hidden(own, second, others, low, stack):
    part, span = own.shape[0], stack.shape[1]
    blocks = (own, second, others.at[:part], others.at[part:])
    offsets = block_offsets(part)
    for k, block in enumerate(blocks):
        place = pl.multiple_of(offsets[k], 16)
        stack[pl.ds(place, part), :] = block[:, low : low + span]


def down_far_kernel(own, second, others, w_down, out, stack):
    stack_hidden(own, second, others, out.shape[0], stack)
    out[...] = dot(stack[...].T, w_down[...]).astype(BF16)


def grad_near_kernel(partial, other, *outs):
    place_blocks(partial[...] + other[...].astype(F32), outs)


def down_near_kernel(own, second, others, w_down, other, *rest):
    stack = rest[-1]
    stack_hidden(own, second, others, 0, stack)
    place_blocks(dot(stack[...].T, w_down[...]) + other[...].astype(F32), rest[:-1])


def add_kernel(*refs):
    terms, outs = refs[:8], refs[8:]
    patches, width = terms[0].shape[0] // 4, terms[0].shape[1]
    for i in range(2):
        total = sum(term[...].astype(F32) for term in terms[4 * i : 4 * i + 4])
        for k, out in enumerate(outs):
            rows = total[k * patches : (k + 1) * patches]
            out[:, i * width : (i + 1) * width] = rows.astype(out.dtype)


def decode_kernel(own, one, two, three, rep, back, weight, owners, partial, outgoing):
    width = rep.shape[1]
    total = own[...] + one[...].astype(F32) + two[...].astype(F32) + three[...].astype(F32)
    states = (total[:, :width] + rep[...].astype(F32)).astype(BF16)
    partial[:, : weight.shape[1]] = dot(states, weight[...]).astype(BF16)
    partial[:, weight.shape[1] :] = (total[:, width:] + back[...]).astype(BF16)
    count = rep.shape[0]
    own_row = jnp.broadcast_to(owners[...], (count, count))
    row = lax.broadcasted_iota(jnp.int32, (count, count), 0)
    column = lax.broadcasted_iota(jnp.int32, (count, count), 1)
    own_column = jnp.sum(jnp.where(row == column, own_row, 0), axis=1, keepdims=True)
    same = jnp.where((own_column == own_row) & (row < column), 1, 0)
    rank = jnp.sum(same, axis=0, keepdims=True)
    targets = 2 * owners[...] + rank
    slots = lax.broadcasted_iota(jnp.int32, (2 * count, count), 0)
    routing = jnp.where(slots == targets, 1.0, 0.0).astype(BF16)
    outgoing[...] = dot(routing, states).astype(BF16)


def finish_kernel(lengths, states, cots, own, one, two, three, out, grad):
    total = (
        own[...].astype(F32) + one[...].astype(F32) + two[...].astype(F32) + three[...].astype(F32)
    )
    pooling, size = membership(lengths[...], states.shape[0])
    width = states.shape[1]
    pick = (((0,), (0,)), ((), ()))
    twice = jnp.concatenate([pooling, pooling], axis=0)
    for values, result, part in (
        (states, out, total[:, :width]),
        (cots, grad, total[:, width:] / size),
    ):
        high = part.astype(BF16)
        low = (part - high.astype(F32)).astype(BF16)
        both = jnp.concatenate([high, low], axis=0)
        spread = lax.dot_general(twice, both, pick, preferred_element_type=F32)
        result[...] = (values[...].astype(F32) + spread).astype(BF16)


def on_device(
    byte_states, patch_lengths, patch_owner, w_enc, w_gate, w_lift, w_down, w_dec, byte_cot
):
    patches = patch_lengths.shape[1]
    width = byte_states.shape[1]
    latent = w_enc.shape[1]
    hid = w_gate.shape[1]
    part = hid // 4
    group = 16 * patches
    owners = patch_owner.reshape(1, patches)
    w_gate, w_lift = w_gate.T, w_lift.T

    def after(value, token):
        return lax.optimization_barrier((value, token))[0]

    def over(swap, own, *sends):
        sends = sends or (own,) * 3
        two, one, three = [swap(sends[k - 1], k) for k in (2, 1, 3)]
        return [own, one, two, three]

    def halve(keep, first):
        own, send = call(
            halve_kernel,
            [shape((keep.shape[0] // 2, width), F32), shape((keep.shape[0] // 2, width), BF16)],
            [keep, first],
            flops=2 * keep.size,
        )
        return own, swap_near(send, False)

    weights = [w_enc, w_gate, w_lift, w_down, w_dec]
    keep, send = call(
        product_kernel,
        [shape((6 * part, width), BF16)] * 2,
        weights,
        flops=6 * hid * width * latent,
        scratch=[pltpu.VMEM(w.shape, BF16) for w in weights]
        + [pltpu.VMEM((3 * hid, width), BF16), pltpu.SemaphoreType.DMA((6,))],
        outside=True,
    )
    first = swap_near(send, True)
    (pooled,) = call(
        pool_kernel,
        [shape((patches, 2 * width), BF16)],
        [patch_lengths, after(byte_states, send), byte_cot],
        flops=4 * patches * byte_states.size,
    )
    (rows,) = call(
        stack_kernel,
        [shape((4 * patches, 2 * width), BF16)],
        over(swap_first, pooled),
        flops=8 * patches * width,
    )
    near = over(swap_second, rows)
    far = [swap_core(block) for block in near]
    own, second = halve(keep, first)
    flops = 4 * group * width * part
    products, near_hidden, near_partial = call(
        near_kernel,
        [
            shape((3 * part, width), BF16),
            shape((part, group), BF16),
            shape((group, width), F32),
        ],
        [*near, own, second],
        flops=3 * flops,
    )
    hidden, far_partial = call(
        far_kernel,
        [shape((part, 2 * group), BF16), shape((group, width), BF16)],
        [*far, products, near_hidden],
        flops=3 * flops,
    )
    hidden_second = swap_near(hidden, False)
    (pair,) = call(pair_kernel, [shape((2 * part, 2 * group), BF16)], [hidden, hidden_second])
    hiddens = [hidden, hidden_second, swap_near(pair, True)]
    grad_terms = call(
        grad_near_kernel,
        [shape((4 * patches, width), BF16)] * 4,
        [near_partial, swap_core(far_partial)],
        flops=near_partial.size,
    )
    grad_first = over(swap_first, *grad_terms)
    patch_rep, back = call(
        encode_kernel,
        [shape((patches, latent), BF16), shape((patches, width), F32)],
        [w_dec, w_enc, pooled],
        flops=6 * patches * width * latent,
    )
    (far_rows,) = call(
        down_far_kernel,
        [shape((group, latent), BF16)],
        [*hiddens, after(w_down, (grad_first[2], back))],
        flops=2 * group * latent * hid,
        scratch=[pltpu.VMEM((hid, group), BF16)],
    )
    terms = call(
        down_near_kernel,
        [shape((4 * patches, latent), BF16)] * 4,
        [*hiddens, w_down, swap_core(far_rows)],
        flops=2 * group * latent * hid,
        scratch=[pltpu.VMEM((hid, group), BF16)],
    )
    own, *sends = call(
        add_kernel,
        [shape((patches, latent + width), F32)] + [shape((patches, latent + width), BF16)] * 3,
        over(swap_first, *terms) + grad_first,
        flops=32 * patches * width,
    )
    partial, outgoing = call(
        decode_kernel,
        [shape((patches, 2 * width), BF16), shape((2 * patches, latent), BF16)],
        [*over(swap_second, own, *sends), patch_rep, back, w_dec, owners],
        flops=2 * patches * width * latent,
    )
    latent_states = lax.all_to_all(outgoing, SEQ, split_axis=0, concat_axis=0, tiled=True)
    partials = over(swap_x, partial)
    byte_out, byte_grad = call(
        finish_kernel,
        [shape(byte_states.shape, BF16), shape(byte_cot.shape, BF16)],
        [patch_lengths, byte_states, byte_cot, *partials],
        flops=16 * patches * byte_states.size,
    )
    return byte_out, byte_grad, latent_states


def solution(mesh):
    fine = Mesh(mesh.devices.reshape(4, 4, 2, 4), ("y", "z", "c", "x"))
    return jax.shard_map(
        on_device,
        mesh=fine,
        in_specs=(
            P(SEQ, None),
            P(SEQ, None),
            P(SEQ, None),
            P(None, "x"),
            P("x", SEQ),
            P("x", SEQ),
            P(SEQ, "x"),
            P("x", None),
            P(SEQ, None),
        ),
        out_specs=(P(SEQ, None), P(SEQ, None), P(SEQ, "x")),
        check_vma=False,
    )
```
